32 devices in a mesh: req: 16 (over z, y, x), head: 2 (over core).
Axes of the slice: x: 2, y: 2, z: 4, core: 2. Of those that a mesh axis runs over, the one named last changes fastest.
Arguments:
- tokens: bfloat16 [80, 1024], P('req'), may hold values from -6 to 6
- norm_gain: float32 [1024], replicated, may hold values from 0.1 to 1.9
- w_qkv: bfloat16 [1024, 8, 384], P(None, 'head'), may hold values from -0.1875 to 0.1875
- persist_kv: bfloat16 [8, 16, 256], P('head'), may hold values from -9 to 9
- memory: bfloat16 [16, 8, 128, 128], P('req', 'head'), may hold values from -0.5 to 0.5
- cache_kv: bfloat16 [128, 512, 8, 256], P('req', None, 'head')
- piece_owner: int32 [128], P('req'), may hold values from 0 to 15, as said below
- piece_len: int32 [128], P('req'), may hold values from 1 to 512, as said below
- w_out: bfloat16 [8, 128, 1024], P('head'), may hold values from -0.1875 to 0.1875
Outputs:
- layer_out: bfloat16 [80, 1024], P('req', 'head')
The draws below stay inside these ranges and needn't reach their ends.
Inputs may be any that keep to these rules, and one draw needn't show every extreme that they name: `piece_owner`: every request owns 1 to 16 pieces, and one request owns exactly 16. `piece_len`: some piece is full.
All inputs are finite; a program needn't handle non-finite values.
Results may differ from the reference program's by a relative error of at most 0.009.
The reference program's roundings to bfloat16 on the way (of `normed`, `query` and `head_out`) count: a program that leaves them out, or rounds other values in their place, can miss the bound.
Values may be sent and summed in bfloat16 or wider, within the bound.
A program may use at most 64 MiB of HBM per device.

```python
import jax
import jax.numpy as jnp
from jax import lax

D = 1024
H = 8
DH = 128
NP = 16
Q = 5
PIECE = 512
MAX_PIECES = 16
REQ_DEV = 1
PIECES_DEV = 8
REQS = 16
SLOTS = 128


def draw_cache_kv(key, part):
    first = jax.random.fold_in(jax.random.fold_in(key, 5), 0)
    shape = (SLOTS, PIECE, H, 2 * DH)
    base = jax.random.normal(first, shape, jnp.float32)
    keys = 2.0 * base[..., :DH]
    values = base[..., DH:]
    return jnp.concatenate([keys, values], axis=-1).astype(jnp.bfloat16)


def draw_piece_owner(key, part):
    first, second, third = jax.random.split(jax.random.fold_in(key, 11), 3)
    spare = PIECES_DEV - REQ_DEV
    devices = SLOTS // PIECES_DEV
    extra = devices * spare
    requests = jnp.arange(REQS, dtype=jnp.int32)
    home_slot = requests // REQ_DEV * PIECES_DEV + requests % REQ_DEV
    spots = jnp.arange(extra, dtype=jnp.int32)
    extra_slot = spots // spare * PIECES_DEV + REQ_DEV + spots % spare
    longest = jax.random.randint(first, (), 0, REQS).astype(jnp.int32)
    others = (longest + 1 + jax.random.permutation(second, REQS - 1).astype(jnp.int32)) % REQS
    later = jnp.maximum(spots - (MAX_PIECES - 1), 0) % (REQS - 1)
    extra_owner = jnp.where(spots < MAX_PIECES - 1, longest, others[later])
    placed = jax.random.permutation(third, extra).astype(jnp.int32)
    owner = jnp.zeros((SLOTS,), jnp.int32).at[home_slot].set(requests)
    owner = owner.at[extra_slot[placed]].set(extra_owner)
    return owner


def draw_piece_len(key, part):
    first, second = jax.random.split(jax.random.fold_in(key, 23), 2)
    lengths = jax.random.randint(first, (SLOTS,), 1, PIECE + 1).astype(jnp.int32)
    where_full = jax.random.randint(second, (), 0, SLOTS)
    return lengths.at[where_full].set(PIECE)


def block_levels(own_key, dims, cuts, low, top_value):
    def one(position, parts):
        heights = jax.random.uniform(jax.random.fold_in(jax.random.fold_in(own_key, 6), position), (parts,), jnp.float32, low / len(cuts), top_value / len(cuts))
        return jnp.repeat(jnp.exp(heights), dims[position] // parts).reshape((-1,) + (1,) * (len(dims) - position - 1))

    factor_of = one(*cuts[0])
    for cut in cuts[1:]:
        factor_of = factor_of * one(*cut)
    return factor_of


def gaussian(stream_key, shape, deviation, bound, cuts=(), kind=jnp.bfloat16):
    gain = block_levels(stream_key, shape, cuts, -0.22, 0.18) if cuts else 1.0
    result = jax.random.normal(stream_key, shape, jnp.float32) * deviation * gain
    return jnp.minimum(jnp.maximum(result, -bound), bound).astype(kind)


def setup_inputs(seed: int = 0) -> dict:
    key_of = jax.random.split(jax.random.key(seed), 10)
    tokens = gaussian(key_of[0], (REQS * Q, D), 1.0, 6.0, ((0, 16),))
    norm_gain = jnp.clip(1.0 + 0.18 * jax.random.normal(key_of[1], (D,), jnp.float32), 0.1, 1.9)
    w_qkv = gaussian(key_of[2], (D, H, 3 * DH), D ** -0.5, 0.1875, ((1, 2),))
    persist_kv = gaussian(key_of[3], (H, NP, 2 * DH), 1.5, 9.0, ((0, 2),))
    memory = gaussian(key_of[4], (REQS, H, DH, DH), DH ** -0.5, 0.5, ((0, 16), (1, 2)))
    cache_kv = draw_cache_kv(jax.random.fold_in(key_of[9], 71), 0)
    piece_owner = draw_piece_owner(jax.random.fold_in(key_of[9], 71), 0)
    piece_len = draw_piece_len(jax.random.fold_in(key_of[9], 71), 0)
    w_out = gaussian(key_of[8], (H, DH, D), (H * DH) ** -0.5, 0.1875, ((0, 2),))
    return dict(tokens=tokens, norm_gain=norm_gain, w_qkv=w_qkv, persist_kv=persist_kv, memory=memory, cache_kv=cache_kv, piece_owner=piece_owner, piece_len=piece_len, w_out=w_out)


masked_score = -1e+30
norm_eps = 1e-06

def reference(tokens, norm_gain, w_qkv, persist_kv, memory, cache_kv, piece_owner, piece_len, w_out):
    f32 = jnp.float32
    xf = tokens.astype(f32)
    normed = (xf * lax.rsqrt(lax.optimization_barrier(jnp.mean(xf * xf, axis=-1, keepdims=True)) + norm_eps) * norm_gain).astype(jnp.bfloat16)
    proj = jnp.einsum('td,dhe->the', normed.astype(f32), w_qkv.astype(f32))
    query = (proj[..., :DH] * DH ** (-0.5)).astype(jnp.bfloat16)
    new_key = proj[..., DH:2 * DH].astype(jnp.bfloat16)
    new_value = proj[..., 2 * DH:].astype(jnp.bfloat16)
    query4 = query.reshape(REQS, Q, H, DH)
    key4 = new_key.reshape(REQS, Q, H, DH)
    value4 = new_value.reshape(REQS, Q, H, DH)

    def slot_part(item):
        block, owner, length = item
        query_rows = lax.dynamic_index_in_dim(query4, owner.astype(jnp.int32), 0, keepdims=False).astype(f32)
        keys = block[..., :DH].astype(f32)
        values = block[..., DH:].astype(f32)
        scores = jnp.einsum('qhe,khe->hqk', query_rows, keys)
        valid = jnp.arange(PIECE) < length
        scores = jnp.where(valid, scores, masked_score)
        peak = lax.optimization_barrier(jnp.max(scores, axis=-1))
        weight = jnp.where(valid, jnp.exp(scores - peak[..., None]), 0.0)
        total = lax.optimization_barrier(jnp.sum(weight, axis=-1))
        rounded = lax.optimization_barrier(weight.astype(jnp.bfloat16)).astype(f32)
        summed = jnp.einsum('hqk,khe->hqe', rounded, values)
        return (peak, total, summed)
    peaks, totals, summed = lax.map(slot_part, (cache_kv, piece_owner, piece_len))
    onehot = piece_owner[:, None] == jnp.arange(REQS, dtype=jnp.int32)[None, :]
    peak_req = lax.optimization_barrier(jnp.max(jnp.where(onehot[:, :, None, None], peaks[:, None], masked_score), axis=0))
    factor = jnp.exp(peaks - peak_req[piece_owner])
    total_cache = jax.ops.segment_sum(totals * factor, piece_owner, num_segments=REQS)
    summed_cache = jax.ops.segment_sum(summed * factor[..., None], piece_owner, num_segments=REQS)
    persist_key = persist_kv[..., :DH].astype(f32)
    persist_value = persist_kv[..., DH:].astype(f32)
    score_persist = jnp.einsum('rqhe,hne->rhqn', query4.astype(f32), persist_key)
    score_new = jnp.einsum('rqhe,rkhe->rhqk', query4.astype(f32), key4.astype(f32))
    causal = jnp.arange(Q)[:, None] >= jnp.arange(Q)[None, :]
    score_new = jnp.where(causal, score_new, masked_score)
    score_own = jnp.concatenate([score_persist, score_new], axis=-1)
    peak_own = lax.optimization_barrier(jnp.max(score_own, axis=-1))
    weight_own = jnp.exp(score_own - peak_own[..., None])
    total_own = lax.optimization_barrier(jnp.sum(weight_own, axis=-1))
    rounded_own = lax.optimization_barrier(weight_own.astype(jnp.bfloat16)).astype(f32)
    summed_own = jnp.einsum('rhqn,hne->rhqe', rounded_own[..., :NP], persist_value)
    summed_own = summed_own + jnp.einsum('rhqk,rkhe->rhqe', rounded_own[..., NP:], value4.astype(f32))
    peak_all = jnp.maximum(peak_req, peak_own)
    scale_cache = jnp.exp(peak_req - peak_all)
    scale_own = jnp.exp(peak_own - peak_all)
    total_all = total_cache * scale_cache + total_own * scale_own
    summed_all = summed_cache * scale_cache[..., None] + summed_own * scale_own[..., None]
    attended = summed_all / total_all[..., None]
    recalled = jnp.einsum('rqhe,rhef->rhqf', query4.astype(f32), memory.astype(f32))
    head_out = (attended + recalled).astype(jnp.bfloat16)
    head_out = jnp.transpose(head_out, (0, 2, 1, 3)).reshape(REQS * Q, H, DH)
    layer_out = jnp.einsum('thd,hdf->tf', head_out.astype(f32), w_out.astype(f32))
    return layer_out.astype(jnp.bfloat16)
```

```python
import functools

import jax
import jax.numpy as jnp
from jax import lax
from jax.experimental import pallas as pl
from jax.experimental.pallas import tpu as pltpu
from jax.sharding import PartitionSpec as P

DH = 128
NP = 16
Q = 5
MESH = pl.DeviceIdType.MESH

masked_score = -1e30
norm_eps = 1e-06
f32 = jnp.float32
bf16 = jnp.bfloat16


def dot(a, b):
    return jnp.dot(a, b, preferred_element_type=f32)


def dot_t(a, b):
    return lax.dot_general(a, b, (((1,), (1,)), ((), ())), preferred_element_type=f32)


def iota(shape, dim):
    return lax.broadcasted_iota(jnp.int32, shape, dim)


def three_terms(x):
    high = x.astype(bf16).astype(f32)
    middle = (x - high).astype(bf16).astype(f32)
    return [high, middle, x - high - middle]


def kernel(
    n, nh, heads, pieces, rows_f, rows,
    qkv_ref, persist_ref, owner_ref, len_ref, cache_ref, memory_ref, w_out_ref,
    out_ref,
    keys, values, memory, w_out, all_query, outbox, inbox, partial, halves,
    key_sem, value_sem, weight_sem, q_send, q_recv, p_send, p_recv, h_send, h_recv,
):
    me = lax.axis_index("req")
    my_head = lax.axis_index("head")
    columns = partial.shape[-1]
    slots = cache_ref.shape[1]

    def cache_copies(s):
        if heads > 1:
            key_view, value_view = cache_ref.at[s, :, 0], cache_ref.at[s, :, 1]
        else:
            key_view, value_view = cache_ref.at[s, :, pl.ds(0, DH)], cache_ref.at[s, :, pl.ds(DH, DH)]
        return (
            pltpu.make_async_copy(key_view, keys.at[s], key_sem.at[s]),
            pltpu.make_async_copy(value_view, values.at[s], value_sem.at[s]),
        )

    memory_copy = pltpu.make_async_copy(memory_ref, memory, weight_sem.at[0])
    w_out_copy = pltpu.make_async_copy(w_out_ref, w_out, weight_sem.at[1])
    memory_copy.start()
    for s in range(pieces):
        for copy in cache_copies(s):
            copy.start()
    w_out_copy.start()

    barrier = pltpu.get_barrier_semaphore()

    @pl.loop(1, n)
    def _(k):
        pl.semaphore_signal(barrier, inc=1, device_id={"req": lax.rem(me + k, n)}, device_id_type=MESH)

    @pl.loop(1, nh)
    def _(k):
        pl.semaphore_signal(barrier, inc=1, device_id={"head": lax.rem(my_head + k, nh)}, device_id_type=MESH)

    all_query[me] = qkv_ref[:, :DH]
    pl.semaphore_wait(barrier, n - 1 + nh - 1)

    def query_copy(slot, other):
        return pltpu.make_async_remote_copy(
            src_ref=all_query.at[slot], dst_ref=all_query.at[slot],
            send_sem=q_send.at[other], recv_sem=q_recv.at[slot],
            device_id={"req": other}, device_id_type=MESH,
        )

    @pl.loop(1, n)
    def _(k):
        query_copy(me, lax.rem(me + k, n)).start()

    query = qkv_ref[:, :DH]
    query_f = query[:rows_f]
    persist = persist_ref[...]
    row = iota((rows_f, 1), 0)
    row_head, row_token = row % heads, row // heads
    col = iota((1, heads * NP), 1)
    score_persist = jnp.where(row_head == col // NP, dot_t(query_f, persist[:, :DH]), masked_score)
    col = iota((1, rows), 1)
    seen = (row_head == col % heads) & (col // heads <= row_token) & (col < Q * heads)
    score_new = jnp.where(seen, dot_t(query_f, qkv_ref[:, DH : 2 * DH]), masked_score)
    m_own = jnp.maximum(
        jnp.max(score_persist, axis=-1, keepdims=True), jnp.max(score_new, axis=-1, keepdims=True)
    )
    w_persist = jnp.exp(score_persist - m_own)
    w_new = jnp.exp(score_new - m_own)
    l_own = jnp.sum(w_persist, axis=-1, keepdims=True) + jnp.sum(w_new, axis=-1, keepdims=True)
    o_own = dot(w_persist.astype(bf16), persist[:, DH:]) + dot(w_new.astype(bf16), qkv_ref[:, 2 * DH :])
    memory_copy.wait()
    recalled = jnp.zeros((rows_f, DH), f32)
    for h in range(heads):
        recalled = jnp.where(row_head == h, dot(query_f, memory[h]), recalled)

    @pl.loop(1, n)
    def _(k):
        query_copy(lax.rem(me + k, n), lax.rem(me + k, n)).wait_recv()

    col = iota((1, slots * heads), 1)
    same_head = row_head == col % heads
    col_slot = col // heads
    key_rows = keys.reshape(pieces, slots * heads, DH)
    value_rows = values.reshape(pieces, slots * heads, DH)
    owners, peaks, totals, sums = [], [], [], []
    for s in range(pieces):
        owner = owner_ref[s]
        key_copy, value_copy = cache_copies(s)
        key_copy.wait()
        valid = same_head & (col_slot < len_ref[s])
        scores = jnp.where(valid, dot_t(all_query[owner][:rows_f], key_rows[s]), masked_score)
        peak = jnp.max(scores, axis=-1, keepdims=True)
        weight = jnp.where(valid, jnp.exp(scores - peak), 0.0)
        value_copy.wait()
        owners.append(owner)
        peaks.append(peak)
        totals.append(jnp.sum(weight, axis=-1, keepdims=True))
        sums.append(dot(weight.astype(bf16), value_rows[s]))

    shared = []
    for s in range(pieces):
        peak = peaks[s]
        for other in range(pieces):
            if other != s:
                peak = jnp.maximum(peak, jnp.where(owners[other] == owners[s], peaks[other], masked_score))
        shared.append(peak)
    for s in range(pieces):
        factor = jnp.exp(peaks[s] - shared[s])
        totals[s] = totals[s] * factor
        sums[s] = sums[s] * factor

    eye = iota((rows_f, DH), 0) == iota((rows_f, DH), 1)
    zeros_tail = jnp.zeros((2, DH), f32)

    def as_row(column):
        return jnp.sum(jnp.where(eye, column, 0.0), axis=0, keepdims=True)

    def message(r):
        m = jnp.full((rows_f, 1), masked_score, f32)
        l = jnp.zeros((rows_f, 1), f32)
        o = jnp.zeros((rows_f, DH), f32)
        for s in range(pieces):
            mine = owners[s] == r
            m = jnp.where(mine, shared[s], m)
            l = l + jnp.where(mine, totals[s], 0.0)
            o = o + jnp.where(mine, sums[s], 0.0)
        tail = three_terms(as_row(m)) + three_terms(as_row(l)) + [zeros_tail]
        return jnp.concatenate([o] + tail, axis=0).astype(bf16)

    def partial_copy(mine, other):
        return pltpu.make_async_remote_copy(
            src_ref=outbox.at[other], dst_ref=inbox.at[mine],
            send_sem=p_send.at[other], recv_sem=p_recv.at[mine],
            device_id={"req": other}, device_id_type=MESH,
        )

    @pl.loop(1, n)
    def _(k):
        other = lax.rem(me + k, n)
        outbox[other] = message(other)
        partial_copy(me, other).start()

    inbox[me] = message(me)

    @pl.loop(1, n)
    def _(k):
        other = lax.rem(me + k, n)
        partial_copy(other, other).wait_recv()

    got = inbox[...].astype(f32)
    tail = got[:, rows_f:]
    m_all = tail[:, 0:1] + (tail[:, 1:2] + tail[:, 2:3])
    l_all = tail[:, 3:4] + (tail[:, 4:5] + tail[:, 5:6])
    m_cache = jnp.max(m_all, axis=0)
    factor = jnp.exp(m_all - m_cache[None])
    l_cache = jnp.sum(l_all * factor, axis=0)

    def as_column(rows_):
        return jnp.sum(jnp.where(eye, rows_, 0.0), axis=-1, keepdims=True)

    o_cache = jnp.zeros((rows_f, DH), f32)
    for k in range(n):
        o_cache = o_cache + got[k, :rows_f] * as_column(factor[k])
    m_cache, l_cache = as_column(m_cache), as_column(l_cache)
    m = jnp.maximum(m_cache, m_own)
    scale_cache, scale_own = jnp.exp(m_cache - m), jnp.exp(m_own - m)
    total = l_cache * scale_cache + l_own * scale_own
    attended = (o_cache * scale_cache + o_own * scale_own) / total
    head_out = (attended + recalled).astype(bf16)

    target, source = iota((8 * heads, rows_f), 0), iota((8 * heads, rows_f), 1)
    pick = (target % 8 < Q) & (source == (target % 8) * heads + target // 8)
    by_head = dot(pick.astype(f32).astype(bf16), head_out)
    lanes = jnp.concatenate([by_head[8 * h : 8 * h + 8] for h in range(heads)], axis=1).astype(bf16)
    w_out_copy.wait()
    layer = dot(lanes, w_out[...].reshape(heads * DH, nh * columns))
    for k in range(nh):
        partial[k] = layer[:, k * columns : (k + 1) * columns]

    def half_copy(mine, other):
        return pltpu.make_async_remote_copy(
            src_ref=partial.at[other], dst_ref=halves.at[mine],
            send_sem=h_send.at[other], recv_sem=h_recv.at[mine],
            device_id={"head": other}, device_id_type=MESH,
        )

    @pl.loop(1, nh)
    def _(k):
        half_copy(my_head, lax.rem(my_head + k, nh)).start()

    halves[my_head] = partial[my_head]

    @pl.loop(1, nh)
    def _(k):
        other = lax.rem(my_head + k, nh)
        half_copy(other, other).wait_recv()

    out_ref[...] = jnp.sum(halves[...], axis=0)[:Q].astype(bf16)

    @pl.loop(1, n)
    def _(k):
        other = lax.rem(me + k, n)
        query_copy(me, other).wait_send()
        partial_copy(me, other).wait_send()

    @pl.loop(1, nh)
    def _(k):
        half_copy(my_head, lax.rem(my_head + k, nh)).wait_send()


def shards(n, nh, tokens, norm_gain, w_qkv, persist_kv, memory, cache_kv, piece_owner, piece_len, w_out):
    heads = w_qkv.shape[1]
    pieces, slots = cache_kv.shape[:2]
    columns = w_out.shape[2] // nh
    rows_f = -(-(Q * heads - 8) // 16) * 16 + 8
    rows = rows_f + 8
    xf = tokens.astype(f32)
    normed = (
        xf * lax.rsqrt(jnp.mean(xf * xf, axis=-1, keepdims=True) + norm_eps) * norm_gain
    ).astype(bf16)
    proj = jnp.einsum("td,dhe->the", normed, w_qkv, preferred_element_type=f32)
    scale = jnp.where(jnp.arange(3 * DH) < DH, DH ** (-0.5), 1.0)
    qkv = (proj * scale).astype(bf16).reshape(Q * heads, 3 * DH)
    qkv = jnp.pad(qkv, ((0, rows - Q * heads), (0, 0)))
    if heads > 1:
        cache = cache_kv.reshape(pieces, slots, heads, 2, DH).transpose(0, 1, 3, 2, 4)
        cache_shape = (pieces, slots, heads, DH)
    else:
        cache = cache_kv.reshape(pieces, slots, 2 * DH)
        cache_shape = (pieces, slots, DH)
    vmem = pl.BlockSpec(memory_space=pltpu.VMEM)
    smem = pl.BlockSpec(memory_space=pltpu.SMEM)
    hbm = pl.BlockSpec(memory_space=pl.ANY)
    dma = pltpu.SemaphoreType.DMA
    return pl.pallas_call(
        functools.partial(kernel, n, nh, heads, pieces, rows_f, rows),
        out_shape=jax.ShapeDtypeStruct((Q, columns), bf16),
        in_specs=[vmem, vmem, smem, smem, hbm, hbm, hbm],
        out_specs=vmem,
        scratch_shapes=[
            pltpu.VMEM(cache_shape, bf16),
            pltpu.VMEM(cache_shape, bf16),
            pltpu.VMEM((heads, DH, DH), bf16),
            pltpu.VMEM((heads, DH, nh * columns), bf16),
            pltpu.VMEM((n, rows, DH), bf16),
            pltpu.VMEM((n, rows, DH), bf16),
            pltpu.VMEM((n, rows, DH), bf16),
            pltpu.VMEM((nh, 8, columns), f32),
            pltpu.VMEM((nh, 8, columns), f32),
            dma((pieces,)), dma((pieces,)), dma((2,)),
            dma((n,)), dma((n,)), dma((n,)), dma((n,)), dma((nh,)), dma((nh,)),
        ],
        compiler_params=pltpu.CompilerParams(
            collective_id=0, has_side_effects=True, vmem_limit_bytes=48 * 2**20
        ),
        cost_estimate=pl.CostEstimate(flops=100_000_000, bytes_accessed=10_000_000, transcendentals=500_000),
    )(
        qkv, persist_kv.reshape(heads * NP, 2 * DH), piece_owner, piece_len, cache,
        memory.reshape(heads, DH, DH), w_out,
    )


def solution(mesh):
    in_specs = (
        P("req", None),
        P(),
        P(None, "head", None),
        P("head", None, None),
        P("req", "head", None, None),
        P("req", None, "head", None),
        P("req"),
        P("req"),
        P("head", None, None),
    )
    n, nh = mesh.shape["req"], mesh.shape["head"]
    return jax.shard_map(
        functools.partial(shards, n, nh), mesh=mesh, in_specs=in_specs, out_specs=P("req", "head"), check_vma=False
    )
```

```python
import functools

import jax
import jax.numpy as jnp
from jax import lax
from jax.experimental import pallas as pl
from jax.experimental.pallas import tpu as pltpu
from jax.sharding import PartitionSpec as P

DH = 128
NP = 16
Q = 5
MESH = pl.DeviceIdType.MESH

masked_score = -1e30
norm_eps = 1e-06
f32 = jnp.float32
bf16 = jnp.bfloat16


def dot(a, b):
    return jnp.dot(a, b, preferred_element_type=f32)


def dot_t(a, b):
    return lax.dot_general(a, b, (((1,), (1,)), ((), ())), preferred_element_type=f32)


def iota(shape, dim):
    return lax.broadcasted_iota(jnp.int32, shape, dim)


def three_terms(x):
    high = x.astype(bf16).astype(f32)
    middle = (x - high).astype(bf16).astype(f32)
    return [high, middle, x - high - middle]


def kernel(
    n, nh, heads, pieces, rows_f, rows,
    owner_ref, len_ref, tokens_ref, gain_ref, w_qkv_ref, persist_ref, cache_ref, memory_ref, w_out_ref,
    out_ref,
    tokens, gain, w_qkv, persist, keys, values, memory, w_out,
    all_query, made, outbox, inbox, partial, halves,
    key_sem, value_sem, weight_sem, w_qkv_sem, q_send, q_recv, p_send, p_recv, h_send, h_recv,
):
    me = lax.axis_index("req")
    my_head = lax.axis_index("head")
    columns = partial.shape[-1]
    slots = cache_ref.shape[1]

    def cache_copies(s):
        if heads > 1:
            key_view, value_view = cache_ref.at[s, :, 0], cache_ref.at[s, :, 1]
        else:
            key_view, value_view = cache_ref.at[s, :, pl.ds(0, DH)], cache_ref.at[s, :, pl.ds(DH, DH)]
        return (
            pltpu.make_async_copy(key_view, keys.at[s], key_sem.at[s]),
            pltpu.make_async_copy(value_view, values.at[s], value_sem.at[s]),
        )

    def w_qkv_copy(c):
        view = w_qkv_ref.at[:, c] if heads > 1 else w_qkv_ref.at[:, pl.ds(c * DH, DH)]
        return pltpu.make_async_copy(view, w_qkv.at[c], w_qkv_sem.at[c])

    tokens_copy = pltpu.make_async_copy(tokens_ref, tokens, weight_sem.at[0])
    gain_copy = pltpu.make_async_copy(gain_ref, gain, weight_sem.at[1])
    persist_copy = pltpu.make_async_copy(persist_ref, persist, weight_sem.at[2])
    memory_copy = pltpu.make_async_copy(memory_ref, memory, weight_sem.at[3])
    w_out_copy = pltpu.make_async_copy(w_out_ref, w_out, weight_sem.at[4])
    tokens_copy.start()
    gain_copy.start()
    for c in range(3):
        w_qkv_copy(c).start()

    barrier = pltpu.get_barrier_semaphore()

    @pl.loop(1, n)
    def _(k):
        pl.semaphore_signal(barrier, inc=1, device_id={"req": lax.rem(me + k, n)}, device_id_type=MESH)

    @pl.loop(1, nh)
    def _(k):
        pl.semaphore_signal(barrier, inc=1, device_id={"head": lax.rem(my_head + k, nh)}, device_id_type=MESH)

    persist_copy.start()
    memory_copy.start()
    for s in range(pieces):
        for copy in cache_copies(s):
            copy.start()
    w_out_copy.start()

    tokens_copy.wait()
    gain_copy.wait()
    x = tokens[...].astype(f32)
    width = x.shape[1]
    normed = (x * lax.rsqrt(jnp.mean(x * x, axis=-1, keepdims=True) + norm_eps) * gain[...]).astype(bf16)
    spread = (iota((rows_f, Q), 0) // heads == iota((rows_f, Q), 1)).astype(f32).astype(bf16)
    repeated = dot(spread, normed)
    if heads > 1:
        blocks = width // DH
        stacked = jnp.concatenate([repeated[:, b * DH : (b + 1) * DH] for b in range(blocks)], axis=0)
        widen = (iota((DH, DH * heads), 0) == iota((DH, DH * heads), 1) // heads).astype(f32).astype(bf16)
        wide = dot(stacked.astype(bf16), widen)
        same = iota((rows_f, DH * heads), 0) % heads == iota((rows_f, DH * heads), 1) % heads
        repeated = jnp.concatenate(
            [jnp.where(same, wide[b * rows_f : (b + 1) * rows_f], 0.0) for b in range(blocks)], axis=1
        )
    repeated = repeated.astype(bf16)
    w_rows = w_qkv.reshape(3, width * heads, DH)

    def project(c, scale):
        w_qkv_copy(c).wait()
        part = dot(repeated, w_rows[c]) * scale
        return jnp.concatenate([part, jnp.zeros((rows - rows_f, DH), f32)], axis=0).astype(bf16)

    query = project(0, DH ** (-0.5))
    all_query[me] = query
    pl.semaphore_wait(barrier, n - 1 + nh - 1)

    def query_copy(slot, other):
        return pltpu.make_async_remote_copy(
            src_ref=all_query.at[slot], dst_ref=all_query.at[slot],
            send_sem=q_send.at[other], recv_sem=q_recv.at[slot],
            device_id={"req": other}, device_id_type=MESH,
        )

    @pl.loop(1, n)
    def _(k):
        query_copy(me, lax.rem(me + k, n)).start()

    new_key = project(1, 1.0)
    new_value = project(2, 1.0)
    query_f = query[:rows_f]
    persist_copy.wait()
    row = iota((rows_f, 1), 0)
    row_head, row_token = row % heads, row // heads
    col = iota((1, heads * NP), 1)
    score_persist = jnp.where(row_head == col // NP, dot_t(query_f, persist[:, :DH]), masked_score)
    col = iota((1, rows), 1)
    seen = (row_head == col % heads) & (col // heads <= row_token) & (col < Q * heads)
    score_new = jnp.where(seen, dot_t(query_f, new_key), masked_score)
    m_own = jnp.maximum(
        jnp.max(score_persist, axis=-1, keepdims=True), jnp.max(score_new, axis=-1, keepdims=True)
    )
    w_persist = jnp.exp(score_persist - m_own)
    w_new = jnp.exp(score_new - m_own)
    l_own = jnp.sum(w_persist, axis=-1, keepdims=True) + jnp.sum(w_new, axis=-1, keepdims=True)
    o_own = dot(w_persist.astype(bf16), persist[:, DH:]) + dot(w_new.astype(bf16), new_value)
    memory_copy.wait()
    recalled = jnp.zeros((rows_f, DH), f32)
    for h in range(heads):
        recalled = jnp.where(row_head == h, dot(query_f, memory[h]), recalled)

    for s in range(pieces):
        for copy in cache_copies(s):
            copy.wait()

    @pl.loop(1, n)
    def _(k):
        query_copy(lax.rem(me + k, n), lax.rem(me + k, n)).wait_recv()

    col = iota((1, slots * heads), 1)
    same_head = row_head == col % heads
    col_slot = col // heads
    key_rows = keys.reshape(pieces, slots * heads, DH)
    value_rows = values.reshape(pieces, slots * heads, DH)
    owners, peaks, totals, sums = [], [], [], []
    for s in range(pieces):
        owner = owner_ref[s]
        valid = same_head & (col_slot < len_ref[s])
        scores = jnp.where(valid, dot_t(all_query[owner][:rows_f], key_rows[s]), masked_score)
        peak = jnp.max(scores, axis=-1, keepdims=True)
        weight = jnp.where(valid, jnp.exp(scores - peak), 0.0)
        owners.append(owner)
        peaks.append(peak)
        totals.append(jnp.sum(weight, axis=-1, keepdims=True))
        sums.append(dot(weight.astype(bf16), value_rows[s]))

    eye = iota((rows_f, DH), 0) == iota((rows_f, DH), 1)
    zeros_tail = jnp.zeros((2, DH), f32)

    def as_row(column):
        return jnp.sum(jnp.where(eye, column, 0.0), axis=0, keepdims=True)

    def send_form(m, l, o):
        return jnp.concatenate([o] + three_terms(m) + three_terms(l) + [zeros_tail], axis=0).astype(bf16)

    same_owner = [[owners[s] == owners[k] for k in range(pieces)] for s in range(pieces)]
    shared = []
    for s in range(pieces):
        peak = peaks[s]
        for k in range(pieces):
            if k != s:
                peak = jnp.maximum(peak, jnp.where(same_owner[s][k], peaks[k], masked_score))
        shared.append(peak)
    peak_rows = [as_row(peak) for peak in shared]
    total_rows = []
    for s in range(pieces):
        factor = jnp.exp(peaks[s] - shared[s])
        total_rows.append(as_row(totals[s] * factor))
        sums[s] = sums[s] * factor
    for s in range(pieces):
        total, summed = total_rows[s], sums[s]
        for k in range(pieces):
            if k != s:
                total = total + jnp.where(same_owner[s][k], total_rows[k], 0.0)
                summed = summed + jnp.where(same_owner[s][k], sums[k], 0.0)
        made[s] = send_form(peak_rows[s], total, summed)
    nothing = jnp.zeros((1, DH), f32)
    made[pieces] = send_form(nothing + masked_score, nothing, jnp.zeros((rows_f, DH), f32))

    def message(r):
        which = jnp.int32(pieces)
        for s in range(pieces):
            which = jnp.where(owners[s] == r, s, which)
        return made[which]

    def partial_copy(mine, other):
        return pltpu.make_async_remote_copy(
            src_ref=outbox.at[other], dst_ref=inbox.at[mine],
            send_sem=p_send.at[other], recv_sem=p_recv.at[mine],
            device_id={"req": other}, device_id_type=MESH,
        )

    @pl.loop(1, n)
    def _(k):
        other = lax.rem(me + k, n)
        outbox[other] = message(other)
        partial_copy(me, other).start()

    inbox[me] = message(me)

    @pl.loop(1, n)
    def _(k):
        other = lax.rem(me + k, n)
        partial_copy(other, other).wait_recv()

    got = inbox[...].astype(f32)
    tail = got[:, rows_f:]
    m_all = tail[:, 0:1] + (tail[:, 1:2] + tail[:, 2:3])
    l_all = tail[:, 3:4] + (tail[:, 4:5] + tail[:, 5:6])
    m_cache = jnp.max(m_all, axis=0)
    factor = jnp.exp(m_all - m_cache[None])
    l_cache = jnp.sum(l_all * factor, axis=0)

    def as_column(rows_):
        return jnp.sum(jnp.where(eye, rows_, 0.0), axis=-1, keepdims=True)

    o_cache = jnp.zeros((rows_f, DH), f32)
    for k in range(n):
        o_cache = o_cache + got[k, :rows_f] * as_column(factor[k])
    m_cache, l_cache = as_column(m_cache), as_column(l_cache)
    m = jnp.maximum(m_cache, m_own)
    scale_cache, scale_own = jnp.exp(m_cache - m), jnp.exp(m_own - m)
    total = l_cache * scale_cache + l_own * scale_own
    attended = (o_cache * scale_cache + o_own * scale_own) / total
    head_out = (attended + recalled).astype(bf16)

    target, source = iota((8 * heads, rows_f), 0), iota((8 * heads, rows_f), 1)
    pick = (target % 8 < Q) & (source == (target % 8) * heads + target // 8)
    by_head = dot(pick.astype(f32).astype(bf16), head_out)
    lanes = jnp.concatenate([by_head[8 * h : 8 * h + 8] for h in range(heads)], axis=1).astype(bf16)
    w_out_copy.wait()
    layer = dot(lanes, w_out[...].reshape(heads * DH, nh * columns))
    for k in range(nh):
        partial[k] = layer[:, k * columns : (k + 1) * columns]

    def half_copy(mine, other):
        return pltpu.make_async_remote_copy(
            src_ref=partial.at[other], dst_ref=halves.at[mine],
            send_sem=h_send.at[other], recv_sem=h_recv.at[mine],
            device_id={"head": other}, device_id_type=MESH,
        )

    @pl.loop(1, nh)
    def _(k):
        half_copy(my_head, lax.rem(my_head + k, nh)).start()

    halves[my_head] = partial[my_head]

    @pl.loop(1, nh)
    def _(k):
        other = lax.rem(my_head + k, nh)
        half_copy(other, other).wait_recv()

    out_ref[...] = jnp.sum(halves[...], axis=0)[:Q].astype(bf16)

    @pl.loop(1, n)
    def _(k):
        other = lax.rem(me + k, n)
        query_copy(me, other).wait_send()
        partial_copy(me, other).wait_send()

    @pl.loop(1, nh)
    def _(k):
        half_copy(my_head, lax.rem(my_head + k, nh)).wait_send()


def shards(n, nh, tokens, norm_gain, w_qkv, persist_kv, memory, cache_kv, piece_owner, piece_len, w_out):
    heads = w_qkv.shape[1]
    pieces, slots = cache_kv.shape[:2]
    columns = w_out.shape[2] // nh
    rows_f = -(-(Q * heads - 8) // 16) * 16 + 8
    rows = rows_f + 8
    width = tokens.shape[1]
    if heads > 1:
        cache = cache_kv.reshape(pieces, slots, heads, 2, DH).transpose(0, 1, 3, 2, 4)
        cache_shape = (pieces, slots, heads, DH)
        w_qkv = w_qkv.reshape(width, heads, 3, DH).transpose(0, 2, 1, 3)
        w_shape = (3, width, heads, DH)
    else:
        cache = cache_kv.reshape(pieces, slots, 2 * DH)
        cache_shape = (pieces, slots, DH)
        w_qkv = w_qkv.reshape(width, 3 * DH)
        w_shape = (3, width, DH)
    vmem = pl.BlockSpec(memory_space=pltpu.VMEM)
    smem = pl.BlockSpec(memory_space=pltpu.SMEM)
    hbm = pl.BlockSpec(memory_space=pltpu.HBM)
    dma = pltpu.SemaphoreType.DMA
    return pl.pallas_call(
        functools.partial(kernel, n, nh, heads, pieces, rows_f, rows),
        out_shape=jax.ShapeDtypeStruct((Q, columns), bf16),
        in_specs=[smem, smem] + [hbm] * 7,
        out_specs=vmem,
        scratch_shapes=[
            pltpu.VMEM((Q, width), bf16),
            pltpu.VMEM((1, width), f32),
            pltpu.VMEM(w_shape, bf16),
            pltpu.VMEM((heads * NP, 2 * DH), bf16),
            pltpu.VMEM(cache_shape, bf16),
            pltpu.VMEM(cache_shape, bf16),
            pltpu.VMEM((heads, DH, DH), bf16),
            pltpu.VMEM((heads, DH, nh * columns), bf16),
            pltpu.VMEM((n, rows, DH), bf16),
            pltpu.VMEM((pieces + 1, rows, DH), bf16),
            pltpu.VMEM((n, rows, DH), bf16),
            pltpu.VMEM((n, rows, DH), bf16),
            pltpu.VMEM((nh, 8, columns), f32),
            pltpu.VMEM((nh, 8, columns), f32),
            dma((pieces,)), dma((pieces,)), dma((5,)), dma((3,)),
            dma((n,)), dma((n,)), dma((n,)), dma((n,)), dma((nh,)), dma((nh,)),
        ],
        compiler_params=pltpu.CompilerParams(
            collective_id=0, has_side_effects=True, vmem_limit_bytes=64 * 2**20 - 16384
        ),
        cost_estimate=pl.CostEstimate(flops=100_000_000, bytes_accessed=10_000_000, transcendentals=500_000),
    )(
        piece_owner, piece_len, tokens, norm_gain.reshape(1, width), w_qkv,
        persist_kv.reshape(heads * NP, 2 * DH), cache, memory.reshape(heads, DH, DH), w_out,
    )


def solution(mesh):
    in_specs = (
        P("req", None),
        P(),
        P(None, "head", None),
        P("head", None, None),
        P("req", "head", None, None),
        P("req", None, "head", None),
        P("req"),
        P("req"),
        P("head", None, None),
    )
    n, nh = mesh.shape["req"], mesh.shape["head"]
    return jax.shard_map(
        functools.partial(shards, n, nh), mesh=mesh, in_specs=in_specs, out_specs=P("req", "head"), check_vma=False
    )
```

```python
import functools

import jax
import jax.numpy as jnp
from jax import lax
from jax.experimental import pallas as pl
from jax.experimental.pallas import tpu as pltpu
from jax.sharding import PartitionSpec as P

DH = 128
NP = 16
Q = 5
MESH = pl.DeviceIdType.MESH

masked_score = -1e30
norm_eps = 1e-06
f32 = jnp.float32
bf16 = jnp.bfloat16


def dot(a, b):
    return jnp.dot(a, b, preferred_element_type=f32)


def dot_t(a, b):
    return lax.dot_general(a, b, (((1,), (1,)), ((), ())), preferred_element_type=f32)


def iota(shape, dim):
    return lax.broadcasted_iota(jnp.int32, shape, dim)


def each(count, body):
    if count <= 16:
        for k in range(1, count):
            body(k)
    else:
        pl.loop(1, count)(body)


def three_terms(x):
    high = x.astype(bf16).astype(f32)
    middle = (x - high).astype(bf16).astype(f32)
    return [high, middle, x - high - middle]


def kernel(
    n, nh, heads, pieces, rows_f, rows,
    owner_ref, len_ref, tokens_ref, gain_ref, w_qkv_ref, persist_ref, cache_ref, memory_ref, w_out_ref,
    out_ref,
    tokens, gain, w_qkv, persist, keys, values, memory, w_out,
    all_query, made, outbox, inbox, partial, halves,
    key_sem, value_sem, weight_sem, w_qkv_sem, q_send, q_recv, p_send, p_recv, h_send, h_recv,
):
    me = lax.axis_index("req")
    my_head = lax.axis_index("head")
    columns = partial.shape[-1]
    slots = cache_ref.shape[1]

    def cache_copies(s):
        if heads > 1:
            key_view, value_view = cache_ref.at[s, :, 0], cache_ref.at[s, :, 1]
        else:
            key_view, value_view = cache_ref.at[s, :, pl.ds(0, DH)], cache_ref.at[s, :, pl.ds(DH, DH)]
        return (
            pltpu.make_async_copy(key_view, keys.at[s], key_sem.at[s]),
            pltpu.make_async_copy(value_view, values.at[s], value_sem.at[s]),
        )

    def w_qkv_copy(c):
        view = w_qkv_ref.at[:, c] if heads > 1 else w_qkv_ref.at[:, pl.ds(c * DH, DH)]
        return pltpu.make_async_copy(view, w_qkv.at[c], w_qkv_sem.at[c])

    tokens_copy = pltpu.make_async_copy(tokens_ref, tokens, weight_sem.at[0])
    gain_copy = pltpu.make_async_copy(gain_ref, gain, weight_sem.at[1])
    persist_copy = pltpu.make_async_copy(persist_ref, persist, weight_sem.at[2])
    memory_copy = pltpu.make_async_copy(memory_ref, memory, weight_sem.at[3])
    w_out_copy = pltpu.make_async_copy(w_out_ref, w_out, weight_sem.at[4])
    tokens_copy.start()
    gain_copy.start()
    for c in range(3):
        w_qkv_copy(c).start()

    barrier = pltpu.get_barrier_semaphore()

    @functools.partial(each, n)
    def _(k):
        pl.semaphore_signal(barrier, inc=1, device_id={"req": lax.rem(me + k, n)}, device_id_type=MESH)

    @functools.partial(each, nh)
    def _(k):
        pl.semaphore_signal(barrier, inc=1, device_id={"head": lax.rem(my_head + k, nh)}, device_id_type=MESH)

    persist_copy.start()
    memory_copy.start()
    for s in range(pieces):
        for copy in cache_copies(s):
            copy.start()
    w_out_copy.start()

    tokens_copy.wait()
    gain_copy.wait()
    x = tokens[...].astype(f32)
    width = x.shape[1]
    normed = (x * lax.rsqrt(jnp.mean(x * x, axis=-1, keepdims=True) + norm_eps) * gain[...]).astype(bf16)
    spread = (iota((rows_f, Q), 0) // heads == iota((rows_f, Q), 1)).astype(f32).astype(bf16)
    repeated = dot(spread, normed)
    if heads > 1:
        blocks = width // DH
        stacked = jnp.concatenate([repeated[:, b * DH : (b + 1) * DH] for b in range(blocks)], axis=0)
        widen = (iota((DH, DH * heads), 0) == iota((DH, DH * heads), 1) // heads).astype(f32).astype(bf16)
        wide = dot(stacked.astype(bf16), widen)
        same = iota((rows_f, DH * heads), 0) % heads == iota((rows_f, DH * heads), 1) % heads
        repeated = jnp.concatenate(
            [jnp.where(same, wide[b * rows_f : (b + 1) * rows_f], 0.0) for b in range(blocks)], axis=1
        )
    repeated = repeated.astype(bf16)
    w_rows = w_qkv.reshape(3, width * heads, DH)

    def project(c, scale):
        w_qkv_copy(c).wait()
        long = width * heads // 4
        parts = [dot(repeated[:, k * long : (k + 1) * long], w_rows[c, k * long : (k + 1) * long]) for k in range(4)]
        part = ((parts[0] + parts[1]) + (parts[2] + parts[3])) * scale
        return jnp.concatenate([part, jnp.zeros((rows - rows_f, DH), f32)], axis=0).astype(bf16)

    query = project(0, DH ** (-0.5))
    all_query[me] = query
    pl.semaphore_wait(barrier, n - 1 + nh - 1)

    def all_others(buffer, send_sem, recv_sem):
        return pltpu.make_async_remote_copy(
            src_ref=buffer.at[pl.ds(0, n - 1)], dst_ref=buffer.at[pl.ds(0, n - 1)],
            send_sem=send_sem, recv_sem=recv_sem,
            device_id={"req": lax.rem(me + 1, n)}, device_id_type=MESH,
        )

    def query_copy(slot, other):
        return pltpu.make_async_remote_copy(
            src_ref=all_query.at[slot], dst_ref=all_query.at[slot],
            send_sem=q_send, recv_sem=q_recv,
            device_id={"req": other}, device_id_type=MESH,
        )

    @functools.partial(each, n)
    def _(k):
        query_copy(me, lax.rem(me + k, n)).start()

    new_key = project(1, 1.0)
    new_value = project(2, 1.0)
    query_f = query[:rows_f]
    persist_copy.wait()
    row = iota((rows_f, 1), 0)
    row_head, row_token = row % heads, row // heads
    col = iota((1, heads * NP), 1)
    score_persist = jnp.where(row_head == col // NP, dot_t(query_f, persist[:, :DH]), masked_score)
    col = iota((1, rows), 1)
    seen = (row_head == col % heads) & (col // heads <= row_token) & (col < Q * heads)
    score_new = jnp.where(seen, dot_t(query_f, new_key), masked_score)
    m_own = jnp.maximum(
        jnp.max(score_persist, axis=-1, keepdims=True), jnp.max(score_new, axis=-1, keepdims=True)
    )
    w_persist = jnp.exp(score_persist - m_own)
    w_new = jnp.exp(score_new - m_own)
    l_own = jnp.sum(w_persist, axis=-1, keepdims=True) + jnp.sum(w_new, axis=-1, keepdims=True)
    o_own = dot(w_persist.astype(bf16), persist[:, DH:]) + dot(w_new.astype(bf16), new_value)
    memory_copy.wait()
    recalled = jnp.zeros((rows_f, DH), f32)
    for h in range(heads):
        recalled = jnp.where(row_head == h, dot(query_f, memory[h]), recalled)

    for s in range(pieces):
        for copy in cache_copies(s):
            copy.wait()

    all_queries = all_others(all_query, q_send, q_recv)
    all_queries.wait_recv()

    col = iota((1, slots * heads), 1)
    same_head = row_head == col % heads
    col_slot = col // heads
    key_rows = keys.reshape(pieces, slots * heads, DH)
    value_rows = values.reshape(pieces, slots * heads, DH)
    owners, peaks, totals, sums = [], [], [], []
    for s in range(pieces):
        owner = owner_ref[s]
        valid = same_head & (col_slot < len_ref[s])
        scores = jnp.where(valid, dot_t(all_query[owner][:rows_f], key_rows[s]), masked_score)
        peak = jnp.max(scores, axis=-1, keepdims=True)
        weight = jnp.where(valid, jnp.exp(scores - peak), 0.0)
        owners.append(owner)
        peaks.append(peak)
        totals.append(jnp.sum(weight, axis=-1, keepdims=True))
        sums.append(dot(weight.astype(bf16), value_rows[s]))

    eye = iota((rows_f, DH), 0) == iota((rows_f, DH), 1)
    zeros_tail = jnp.zeros((2, DH), f32)

    def as_row(column):
        return jnp.sum(jnp.where(eye, column, 0.0), axis=0, keepdims=True)

    def send_form(m, l, o):
        return jnp.concatenate([o] + three_terms(m) + three_terms(l) + [zeros_tail], axis=0).astype(bf16)

    same_owner = [[owners[s] == owners[k] for k in range(pieces)] for s in range(pieces)]
    shared = []
    for s in range(pieces):
        peak = peaks[s]
        for k in range(pieces):
            if k != s:
                peak = jnp.maximum(peak, jnp.where(same_owner[s][k], peaks[k], masked_score))
        shared.append(peak)
    peak_rows = [as_row(peak) for peak in shared]
    total_rows = []
    for s in range(pieces):
        factor = jnp.exp(peaks[s] - shared[s])
        total_rows.append(as_row(totals[s] * factor))
        sums[s] = sums[s] * factor
    for s in range(pieces):
        total, summed = total_rows[s], sums[s]
        for k in range(pieces):
            if k != s:
                total = total + jnp.where(same_owner[s][k], total_rows[k], 0.0)
                summed = summed + jnp.where(same_owner[s][k], sums[k], 0.0)
        made[s] = send_form(peak_rows[s], total, summed)
    nothing = jnp.zeros((1, DH), f32)
    made[pieces] = send_form(nothing + masked_score, nothing, jnp.zeros((rows_f, DH), f32))

    def message(r):
        which = jnp.int32(pieces)
        for s in range(pieces):
            which = jnp.where(owners[s] == r, s, which)
        return made[which]

    def partial_copy(mine, other):
        return pltpu.make_async_remote_copy(
            src_ref=outbox.at[other], dst_ref=inbox.at[mine],
            send_sem=p_send, recv_sem=p_recv,
            device_id={"req": other}, device_id_type=MESH,
        )

    @functools.partial(each, n)
    def _(k):
        other = lax.rem(me + k, n)
        outbox[other] = message(other)
        partial_copy(me, other).start()

    inbox[me] = message(me)

    all_partials = all_others(inbox, p_send, p_recv)
    all_partials.wait_recv()

    got = inbox[...].astype(f32)
    tail = got[:, rows_f:]
    m_all = tail[:, 0:1] + (tail[:, 1:2] + tail[:, 2:3])
    l_all = tail[:, 3:4] + (tail[:, 4:5] + tail[:, 5:6])
    m_cache = jnp.max(m_all, axis=0)
    factor = jnp.exp(m_all - m_cache[None])
    l_cache = jnp.sum(l_all * factor, axis=0)

    def as_column(rows_):
        return jnp.sum(jnp.where(eye, rows_, 0.0), axis=-1, keepdims=True)

    o_cache = jnp.zeros((rows_f, DH), f32)
    for k in range(n):
        o_cache = o_cache + got[k, :rows_f] * as_column(factor[k])
    m_cache, l_cache = as_column(m_cache), as_column(l_cache)
    m = jnp.maximum(m_cache, m_own)
    scale_cache, scale_own = jnp.exp(m_cache - m), jnp.exp(m_own - m)
    total = l_cache * scale_cache + l_own * scale_own
    attended = (o_cache * scale_cache + o_own * scale_own) / total
    head_out = (attended + recalled).astype(bf16)

    target, source = iota((8 * heads, rows_f), 0), iota((8 * heads, rows_f), 1)
    pick = (target % 8 < Q) & (source == (target % 8) * heads + target // 8)
    by_head = dot(pick.astype(f32).astype(bf16), head_out)
    lanes = jnp.concatenate([by_head[8 * h : 8 * h + 8] for h in range(heads)], axis=1).astype(bf16)
    w_out_copy.wait()
    layer = dot(lanes, w_out[...].reshape(heads * DH, nh * columns))
    for k in range(nh):
        partial[k] = layer[:, k * columns : (k + 1) * columns]

    def half_copy(mine, other):
        return pltpu.make_async_remote_copy(
            src_ref=partial.at[other], dst_ref=halves.at[mine],
            send_sem=h_send.at[other], recv_sem=h_recv.at[mine],
            device_id={"head": other}, device_id_type=MESH,
        )

    @functools.partial(each, nh)
    def _(k):
        half_copy(my_head, lax.rem(my_head + k, nh)).start()

    halves[my_head] = partial[my_head]

    @functools.partial(each, nh)
    def _(k):
        other = lax.rem(my_head + k, nh)
        half_copy(other, other).wait_recv()

    out_ref[...] = jnp.sum(halves[...], axis=0)[:Q].astype(bf16)

    all_queries.wait_send()
    all_partials.wait_send()

    @functools.partial(each, nh)
    def _(k):
        half_copy(my_head, lax.rem(my_head + k, nh)).wait_send()


def shards(n, nh, tokens, norm_gain, w_qkv, persist_kv, memory, cache_kv, piece_owner, piece_len, w_out):
    heads = w_qkv.shape[1]
    pieces, slots = cache_kv.shape[:2]
    columns = w_out.shape[2] // nh
    rows_f = -(-(Q * heads - 8) // 16) * 16 + 8
    rows = rows_f + 8
    width = tokens.shape[1]
    if heads > 1:
        cache = cache_kv.reshape(pieces, slots, heads, 2, DH).transpose(0, 1, 3, 2, 4)
        cache_shape = (pieces, slots, heads, DH)
        w_qkv = w_qkv.reshape(width, heads, 3, DH).transpose(0, 2, 1, 3)
        w_shape = (3, width, heads, DH)
    else:
        cache = cache_kv.reshape(pieces, slots, 2 * DH)
        cache_shape = (pieces, slots, DH)
        w_qkv = w_qkv.reshape(width, 3 * DH)
        w_shape = (3, width, DH)
    vmem = pl.BlockSpec(memory_space=pltpu.VMEM)
    smem = pl.BlockSpec(memory_space=pltpu.SMEM)
    hbm = pl.BlockSpec(memory_space=pltpu.HBM)
    dma = pltpu.SemaphoreType.DMA
    return pl.pallas_call(
        functools.partial(kernel, n, nh, heads, pieces, rows_f, rows),
        out_shape=pltpu.VMEM((Q, columns), bf16),
        in_specs=[smem, smem] + [hbm] * 7,
        out_specs=vmem,
        scratch_shapes=[
            pltpu.VMEM((Q, width), bf16),
            pltpu.VMEM((1, width), f32),
            pltpu.VMEM(w_shape, bf16),
            pltpu.VMEM((heads * NP, 2 * DH), bf16),
            pltpu.VMEM(cache_shape, bf16),
            pltpu.VMEM(cache_shape, bf16),
            pltpu.VMEM((heads, DH, DH), bf16),
            pltpu.VMEM((heads, DH, nh * columns), bf16),
            pltpu.VMEM((n, rows, DH), bf16),
            pltpu.VMEM((pieces + 1, rows, DH), bf16),
            pltpu.VMEM((n, rows, DH), bf16),
            pltpu.VMEM((n, rows, DH), bf16),
            pltpu.VMEM((nh, 8, columns), f32),
            pltpu.VMEM((nh, 8, columns), f32),
            dma((pieces,)), dma((pieces,)), dma((5,)), dma((3,)),
            dma, dma, dma, dma, dma((nh,)), dma((nh,)),
        ],
        compiler_params=pltpu.CompilerParams(
            collective_id=0, has_side_effects=True, vmem_limit_bytes=62 * 2**20
        ),
        cost_estimate=pl.CostEstimate(flops=100_000_000, bytes_accessed=10_000_000, transcendentals=500_000),
    )(
        piece_owner, piece_len, tokens, norm_gain.reshape(1, width), w_qkv,
        persist_kv.reshape(heads * NP, 2 * DH), cache, memory.reshape(heads, DH, DH), w_out,
    )


def solution(mesh):
    in_specs = (
        P("req", None),
        P(),
        P(None, "head", None),
        P("head", None, None),
        P("req", "head", None, None),
        P("req", None, "head", None),
        P("req"),
        P("req"),
        P("head", None, None),
    )
    n, nh = mesh.shape["req"], mesh.shape["head"]
    return jax.shard_map(
        functools.partial(shards, n, nh), mesh=mesh, in_specs=in_specs, out_specs=P("req", "head"), check_vma=False
    )
```

```python
import functools

import jax
import jax.numpy as jnp
from jax import lax
from jax.experimental import pallas as pl
from jax.experimental.pallas import tpu as pltpu
from jax.sharding import PartitionSpec as P

DH = 128
NP = 16
Q = 5
MESH = pl.DeviceIdType.MESH

masked_score = -1e30
norm_eps = 1e-06
f32 = jnp.float32
bf16 = jnp.bfloat16


def dot(a, b):
    return jnp.dot(a, b, preferred_element_type=f32)


def dot_t(a, b):
    return lax.dot_general(a, b, (((1,), (1,)), ((), ())), preferred_element_type=f32)


def iota(shape, dim):
    return lax.broadcasted_iota(jnp.int32, shape, dim)


def each(count, body):
    if count <= 16:
        for k in range(1, count):
            body(k)
    else:
        pl.loop(1, count)(body)


def three_terms(x):
    high = x.astype(bf16).astype(f32)
    middle = (x - high).astype(bf16).astype(f32)
    return [high, middle, x - high - middle]


def kernel(
    n, nh, heads, pieces, rows_f, rows,
    owner_ref, len_ref, tokens_ref, gain_ref, w_qkv_ref, persist_ref, cache_ref, memory_ref, w_out_ref,
    out_ref,
    tokens, gain, w_qkv, persist, keys, values, memory, w_out,
    all_query, made, outbox, inbox, partial, halves,
    key_sem, value_sem, weight_sem, w_qkv_sem, q_send, q_recv, p_send, p_recv, h_send, h_recv,
):
    me = lax.axis_index("req")
    my_head = lax.axis_index("head")
    columns = partial.shape[-1]
    slots = cache_ref.shape[1]

    def cache_copies(s):
        if heads > 1:
            key_view, value_view = cache_ref.at[s, :, 0], cache_ref.at[s, :, 1]
        else:
            key_view, value_view = cache_ref.at[s, :, pl.ds(0, DH)], cache_ref.at[s, :, pl.ds(DH, DH)]
        return (
            pltpu.make_async_copy(key_view, keys.at[s], key_sem.at[s]),
            pltpu.make_async_copy(value_view, values.at[s], value_sem.at[s]),
        )

    def w_qkv_copy(c):
        view = w_qkv_ref.at[:, c] if heads > 1 else w_qkv_ref.at[:, pl.ds(c * DH, DH)]
        return pltpu.make_async_copy(view, w_qkv.at[c], w_qkv_sem.at[c])

    tokens_copy = pltpu.make_async_copy(tokens_ref, tokens, weight_sem.at[0])
    gain_copy = pltpu.make_async_copy(gain_ref, gain, weight_sem.at[1])
    persist_copy = pltpu.make_async_copy(persist_ref, persist, weight_sem.at[2])
    memory_copy = pltpu.make_async_copy(memory_ref, memory, weight_sem.at[3])
    w_out_copy = pltpu.make_async_copy(w_out_ref, w_out, weight_sem.at[4])
    tokens_copy.start()
    gain_copy.start()
    for c in range(3):
        w_qkv_copy(c).start()

    barrier = pltpu.get_barrier_semaphore()

    @functools.partial(each, n)
    def _(k):
        pl.semaphore_signal(barrier, inc=1, device_id={"req": lax.rem(me + k, n)}, device_id_type=MESH)

    @functools.partial(each, nh)
    def _(k):
        pl.semaphore_signal(barrier, inc=1, device_id={"head": lax.rem(my_head + k, nh)}, device_id_type=MESH)

    persist_copy.start()
    memory_copy.start()
    for s in range(pieces):
        for copy in cache_copies(s):
            copy.start()
    w_out_copy.start()

    tokens_copy.wait()
    gain_copy.wait()
    x = tokens[...].astype(f32)
    width = x.shape[1]
    normed = (x * lax.rsqrt(jnp.mean(x * x, axis=-1, keepdims=True) + norm_eps) * gain[...]).astype(bf16)
    spread = (iota((rows_f, Q), 0) // heads == iota((rows_f, Q), 1)).astype(f32).astype(bf16)
    repeated = dot(spread, normed)
    if heads > 1:
        blocks = width // DH
        stacked = jnp.concatenate([repeated[:, b * DH : (b + 1) * DH] for b in range(blocks)], axis=0)
        widen = (iota((DH, DH * heads), 0) == iota((DH, DH * heads), 1) // heads).astype(f32).astype(bf16)
        wide = dot(stacked.astype(bf16), widen)
        same = iota((rows_f, DH * heads), 0) % heads == iota((rows_f, DH * heads), 1) % heads
        repeated = jnp.concatenate(
            [jnp.where(same, wide[b * rows_f : (b + 1) * rows_f], 0.0) for b in range(blocks)], axis=1
        )
    repeated = repeated.astype(bf16)
    w_rows = w_qkv.reshape(3, width * heads, DH)

    def project(c, scale):
        w_qkv_copy(c).wait()
        long = width * heads // 4
        parts = [dot(repeated[:, k * long : (k + 1) * long], w_rows[c, k * long : (k + 1) * long]) for k in range(4)]
        part = ((parts[0] + parts[1]) + (parts[2] + parts[3])) * scale
        return jnp.concatenate([part, jnp.zeros((rows - rows_f, DH), f32)], axis=0).astype(bf16)

    query = project(0, DH ** (-0.5))
    all_query[me] = query
    pl.semaphore_wait(barrier, n - 1 + nh - 1)

    def all_others(buffer, send_sem, recv_sem):
        return pltpu.make_async_remote_copy(
            src_ref=buffer.at[pl.ds(0, n - 1)], dst_ref=buffer.at[pl.ds(0, n - 1)],
            send_sem=send_sem, recv_sem=recv_sem,
            device_id={"req": lax.rem(me + 1, n)}, device_id_type=MESH,
        )

    def query_copy(slot, other):
        return pltpu.make_async_remote_copy(
            src_ref=all_query.at[slot], dst_ref=all_query.at[slot],
            send_sem=q_send, recv_sem=q_recv,
            device_id={"req": other}, device_id_type=MESH,
        )

    @functools.partial(each, n)
    def _(k):
        query_copy(me, lax.rem(me + k, n)).start()

    query_f = query[:rows_f]
    row = iota((rows_f, 1), 0)
    row_head, row_token = row % heads, row // heads
    memory_copy.wait()
    recalled = jnp.zeros((rows_f, DH), f32)
    for h in range(heads):
        recalled = jnp.where(row_head == h, dot(query_f, memory[h]), recalled)
    persist_copy.wait()
    col = iota((1, heads * NP), 1)
    score_persist = jnp.where(row_head == col // NP, dot_t(query_f, persist[:, :DH]), masked_score)

    for s in range(pieces):
        for copy in cache_copies(s):
            copy.wait()

    all_queries = all_others(all_query, q_send, q_recv)
    all_queries.wait_recv()

    col = iota((1, slots * heads), 1)
    same_head = row_head == col % heads
    col_slot = col // heads
    key_rows = keys.reshape(pieces, slots * heads, DH)
    value_rows = values.reshape(pieces, slots * heads, DH)
    owners = [owner_ref[s] for s in range(pieces)]
    peaks, totals, sums = [], [], []
    gap = jnp.zeros((rows_f, DH), f32)
    for s in range(0, pieces, 2):
        pair = (s, s + 1)
        first, second = [all_query[owners[k]].astype(f32)[:rows_f] for k in pair]
        left = jnp.concatenate([first, gap], axis=0)
        right = jnp.concatenate([gap, second], axis=0)
        both = jnp.concatenate([left, right], axis=1).astype(bf16)
        scores = dot_t(both, jnp.concatenate([key_rows[k] for k in pair], axis=1))
        weights = []
        for k in pair:
            valid = same_head & (col_slot < len_ref[k])
            own_scores = jnp.where(valid, scores[(k - s) * rows_f : (k - s + 1) * rows_f], masked_score)
            peak = jnp.max(own_scores, axis=-1, keepdims=True)
            weight = jnp.where(valid, jnp.exp(own_scores - peak), 0.0)
            peaks.append(peak)
            totals.append(jnp.sum(weight, axis=-1, keepdims=True))
            weights.append(weight)
        weights = jnp.concatenate(weights, axis=0).astype(bf16)
        summed = dot(weights, jnp.concatenate([value_rows[k] for k in pair], axis=1))
        sums += [summed[:rows_f, :DH], summed[rows_f:, DH:]]

    eye = iota((rows_f, DH), 0) == iota((rows_f, DH), 1)
    zeros_tail = jnp.zeros((2, DH), f32)

    def as_row(column):
        return jnp.sum(jnp.where(eye, column, 0.0), axis=0, keepdims=True)

    def send_form(m, l, o):
        return jnp.concatenate([o] + three_terms(m) + three_terms(l) + [zeros_tail], axis=0).astype(bf16)

    same_owner = [[owners[s] == owners[k] for k in range(pieces)] for s in range(pieces)]
    shared = []
    for s in range(pieces):
        peak = peaks[s]
        for k in range(pieces):
            if k != s:
                peak = jnp.maximum(peak, jnp.where(same_owner[s][k], peaks[k], masked_score))
        shared.append(peak)
    peak_rows = [as_row(peak) for peak in shared]
    total_rows = []
    for s in range(pieces):
        factor = jnp.exp(peaks[s] - shared[s])
        total_rows.append(as_row(totals[s] * factor))
        sums[s] = sums[s] * factor
    for s in range(pieces):
        total, summed = total_rows[s], sums[s]
        for k in range(pieces):
            if k != s:
                total = total + jnp.where(same_owner[s][k], total_rows[k], 0.0)
                summed = summed + jnp.where(same_owner[s][k], sums[k], 0.0)
        made[s] = send_form(peak_rows[s], total, summed)
    nothing = jnp.zeros((1, DH), f32)
    made[pieces] = send_form(nothing + masked_score, nothing, jnp.zeros((rows_f, DH), f32))

    def message(r):
        which = jnp.int32(pieces)
        for s in range(pieces):
            which = jnp.where(owners[s] == r, s, which)
        return made[which]

    def partial_copy(mine, other):
        return pltpu.make_async_remote_copy(
            src_ref=outbox.at[other], dst_ref=inbox.at[mine],
            send_sem=p_send, recv_sem=p_recv,
            device_id={"req": other}, device_id_type=MESH,
        )

    @functools.partial(each, n)
    def _(k):
        other = lax.rem(me + k, n)
        outbox[other] = message(other)
        partial_copy(me, other).start()

    inbox[me] = message(me)

    new_key = project(1, 1.0)
    new_value = project(2, 1.0)
    col = iota((1, rows), 1)
    seen = (row_head == col % heads) & (col // heads <= row_token) & (col < Q * heads)
    score_new = jnp.where(seen, dot_t(query_f, new_key), masked_score)
    m_own = jnp.maximum(
        jnp.max(score_persist, axis=-1, keepdims=True), jnp.max(score_new, axis=-1, keepdims=True)
    )
    w_persist = jnp.exp(score_persist - m_own)
    w_new = jnp.exp(score_new - m_own)
    l_own = jnp.sum(w_persist, axis=-1, keepdims=True) + jnp.sum(w_new, axis=-1, keepdims=True)
    o_own = dot(w_persist.astype(bf16), persist[:, DH:]) + dot(w_new.astype(bf16), new_value)

    all_partials = all_others(inbox, p_send, p_recv)
    all_partials.wait_recv()

    got = inbox[...].astype(f32)
    tail = got[:, rows_f:]
    m_all = tail[:, 0:1] + (tail[:, 1:2] + tail[:, 2:3])
    l_all = tail[:, 3:4] + (tail[:, 4:5] + tail[:, 5:6])
    m_cache = jnp.max(m_all, axis=0)
    factor = jnp.exp(m_all - m_cache[None])
    l_cache = jnp.sum(l_all * factor, axis=0)

    def as_column(rows_):
        return jnp.sum(jnp.where(eye, rows_, 0.0), axis=-1, keepdims=True)

    o_cache = jnp.zeros((rows_f, DH), f32)
    for k in range(n):
        o_cache = o_cache + got[k, :rows_f] * as_column(factor[k])
    m_cache, l_cache = as_column(m_cache), as_column(l_cache)
    m = jnp.maximum(m_cache, m_own)
    scale_cache, scale_own = jnp.exp(m_cache - m), jnp.exp(m_own - m)
    total = l_cache * scale_cache + l_own * scale_own
    attended = (o_cache * scale_cache + o_own * scale_own) / total
    head_out = (attended + recalled).astype(bf16)

    target, source = iota((8 * heads, rows_f), 0), iota((8 * heads, rows_f), 1)
    pick = (target % 8 < Q) & (source == (target % 8) * heads + target // 8)
    by_head = dot(pick.astype(f32).astype(bf16), head_out)
    lanes = jnp.concatenate([by_head[8 * h : 8 * h + 8] for h in range(heads)], axis=1).astype(bf16)
    w_out_copy.wait()
    def half_copy(mine, other):
        return pltpu.make_async_remote_copy(
            src_ref=partial.at[other], dst_ref=halves.at[mine],
            send_sem=h_send.at[other], recv_sem=h_recv.at[mine],
            device_id={"head": other}, device_id_type=MESH,
        )

    def layer_part(k):
        start = pl.multiple_of(k * columns, columns)
        return dot(lanes, w_out[:, :, pl.ds(start, columns)].reshape(heads * DH, columns))

    @functools.partial(each, nh)
    def _(k):
        other = lax.rem(my_head + k, nh)
        partial[other] = layer_part(other)
        half_copy(my_head, other).start()

    halves[my_head] = layer_part(my_head)

    @functools.partial(each, nh)
    def _(k):
        other = lax.rem(my_head + k, nh)
        half_copy(other, other).wait_recv()

    out_ref[...] = jnp.sum(halves[...], axis=0)[:Q].astype(bf16)

    all_queries.wait_send()
    all_partials.wait_send()

    @functools.partial(each, nh)
    def _(k):
        half_copy(my_head, lax.rem(my_head + k, nh)).wait_send()


def shards(n, nh, tokens, norm_gain, w_qkv, persist_kv, memory, cache_kv, piece_owner, piece_len, w_out):
    heads = w_qkv.shape[1]
    pieces, slots = cache_kv.shape[:2]
    columns = w_out.shape[2] // nh
    rows_f = -(-(Q * heads - 8) // 16) * 16 + 8
    rows = rows_f + 8
    width = tokens.shape[1]
    if heads > 1:
        cache = cache_kv.reshape(pieces, slots, heads, 2, DH).transpose(0, 1, 3, 2, 4)
        cache_shape = (pieces, slots, heads, DH)
        w_qkv = w_qkv.reshape(width, heads, 3, DH).transpose(0, 2, 1, 3)
        w_shape = (3, width, heads, DH)
    else:
        cache = cache_kv.reshape(pieces, slots, 2 * DH)
        cache_shape = (pieces, slots, DH)
        w_qkv = w_qkv.reshape(width, 3 * DH)
        w_shape = (3, width, DH)
    vmem = pl.BlockSpec(memory_space=pltpu.VMEM)
    smem = pl.BlockSpec(memory_space=pltpu.SMEM)
    hbm = pl.BlockSpec(memory_space=pltpu.HBM)
    dma = pltpu.SemaphoreType.DMA
    return pl.pallas_call(
        functools.partial(kernel, n, nh, heads, pieces, rows_f, rows),
        out_shape=pltpu.VMEM((Q, columns), bf16),
        in_specs=[smem, smem] + [hbm] * 7,
        out_specs=vmem,
        scratch_shapes=[
            pltpu.VMEM((Q, width), bf16),
            pltpu.VMEM((1, width), f32),
            pltpu.VMEM(w_shape, bf16),
            pltpu.VMEM((heads * NP, 2 * DH), bf16),
            pltpu.VMEM(cache_shape, bf16),
            pltpu.VMEM(cache_shape, bf16),
            pltpu.VMEM((heads, DH, DH), bf16),
            pltpu.VMEM((heads, DH, nh * columns), bf16),
            pltpu.VMEM((n, rows, DH), bf16),
            pltpu.VMEM((pieces + 1, rows, DH), bf16),
            pltpu.VMEM((n, rows, DH), bf16),
            pltpu.VMEM((n, rows, DH), bf16),
            pltpu.VMEM((nh, 8, columns), f32),
            pltpu.VMEM((nh, 8, columns), f32),
            dma((pieces,)), dma((pieces,)), dma((5,)), dma((3,)),
            dma, dma, dma, dma, dma((nh,)), dma((nh,)),
        ],
        compiler_params=pltpu.CompilerParams(
            collective_id=0, has_side_effects=True, vmem_limit_bytes=62 * 2**20
        ),
        cost_estimate=pl.CostEstimate(flops=100_000_000, bytes_accessed=10_000_000, transcendentals=500_000),
    )(
        piece_owner, piece_len, tokens, norm_gain.reshape(1, width), w_qkv,
        persist_kv.reshape(heads * NP, 2 * DH), cache, memory.reshape(heads, DH, DH), w_out,
    )


def solution(mesh):
    in_specs = (
        P("req", None),
        P(),
        P(None, "head", None),
        P("head", None, None),
        P("req", "head", None, None),
        P("req", None, "head", None),
        P("req"),
        P("req"),
        P("head", None, None),
    )
    n, nh = mesh.shape["req"], mesh.shape["head"]
    return jax.shard_map(
        functools.partial(shards, n, nh), mesh=mesh, in_specs=in_specs, out_specs=P("req", "head"), check_vma=False
    )
```

```python
import functools

import jax
import jax.numpy as jnp
from jax import lax
from jax.experimental import pallas as pl
from jax.experimental.pallas import tpu as pltpu
from jax.sharding import PartitionSpec as P

DH = 128
NP = 16
Q = 5
MESH = pl.DeviceIdType.MESH

masked_score = -1e30
norm_eps = 1e-06
f32 = jnp.float32
bf16 = jnp.bfloat16


def dot(a, b):
    return jnp.dot(a, b, preferred_element_type=f32)


def dot_t(a, b):
    return lax.dot_general(a, b, (((1,), (1,)), ((), ())), preferred_element_type=f32)


def iota(shape, dim):
    return lax.broadcasted_iota(jnp.int32, shape, dim)


def each(count, body):
    if count <= 16:
        for k in sorted(range(1, count), key=lambda k: abs(2 * k - count)):
            body(k)
    else:
        pl.loop(1, count)(body)


def three_terms(x):
    high = x.astype(bf16).astype(f32)
    middle = (x - high).astype(bf16).astype(f32)
    return [high, middle, x - high - middle]


def kernel(
    n, nh, heads, pieces, rows_f, rows,
    owner_hbm, len_hbm, tokens_ref, gain_ref, w_qkv_ref, persist_ref, cache_ref, memory_ref, w_out_ref,
    out_ref,
    owner_ref, len_ref, tokens, gain, w_qkv, persist, keys, values, memory, w_out,
    all_query, made, outbox, inbox, partial, halves,
    key_sem, value_sem, weight_sem, w_qkv_sem, q_send, q_recv, p_send, p_recv, h_send, h_recv,
):
    me = lax.axis_index("req")
    my_head = lax.axis_index("head")
    columns = partial.shape[-1]
    slots = cache_ref.shape[1]

    barrier = pltpu.get_barrier_semaphore()

    @functools.partial(each, n)
    def _(k):
        pl.semaphore_signal(barrier, inc=1, device_id={"req": lax.rem(me + k, n)}, device_id_type=MESH)

    @functools.partial(each, nh)
    def _(k):
        pl.semaphore_signal(barrier, inc=1, device_id={"head": lax.rem(my_head + k, nh)}, device_id_type=MESH)

    def cache_copies(s):
        if heads > 1:
            key_view, value_view = cache_ref.at[s, :, 0], cache_ref.at[s, :, 1]
        else:
            key_view, value_view = cache_ref.at[s, :, pl.ds(0, DH)], cache_ref.at[s, :, pl.ds(DH, DH)]
        return (
            pltpu.make_async_copy(key_view, keys.at[s], key_sem.at[s]),
            pltpu.make_async_copy(value_view, values.at[s], value_sem.at[s]),
        )

    def w_qkv_copy(c):
        view = w_qkv_ref.at[:, c] if heads > 1 else w_qkv_ref.at[:, pl.ds(c * DH, DH)]
        return pltpu.make_async_copy(view, w_qkv.at[c], w_qkv_sem.at[c])

    tokens_copy = pltpu.make_async_copy(tokens_ref, tokens, weight_sem.at[0])
    gain_copy = pltpu.make_async_copy(gain_ref, gain, weight_sem.at[1])
    persist_copy = pltpu.make_async_copy(persist_ref, persist, weight_sem.at[2])
    memory_copy = pltpu.make_async_copy(memory_ref, memory, weight_sem.at[3])
    w_out_copy = pltpu.make_async_copy(w_out_ref, w_out, weight_sem.at[4])
    tokens_copy.start()
    gain_copy.start()
    for c in range(3):
        w_qkv_copy(c).start()

    owner_copy = pltpu.make_async_copy(owner_hbm, owner_ref, weight_sem.at[5])
    len_copy = pltpu.make_async_copy(len_hbm, len_ref, weight_sem.at[6])
    owner_copy.start()
    len_copy.start()
    persist_copy.start()
    memory_copy.start()
    for s in range(pieces):
        for copy in cache_copies(s):
            copy.start()
    w_out_copy.start()

    tokens_copy.wait()
    gain_copy.wait()
    x = tokens[...].astype(f32)
    width = x.shape[1]
    normed = (x * lax.rsqrt(jnp.mean(x * x, axis=-1, keepdims=True) + norm_eps) * gain[...]).astype(bf16)
    spread = (iota((rows_f, Q), 0) // heads == iota((rows_f, Q), 1)).astype(f32).astype(bf16)
    repeated = dot(spread, normed)
    if heads > 1:
        blocks = width // DH
        stacked = jnp.concatenate([repeated[:, b * DH : (b + 1) * DH] for b in range(blocks)], axis=0)
        widen = (iota((DH, DH * heads), 0) == iota((DH, DH * heads), 1) // heads).astype(f32).astype(bf16)
        wide = dot(stacked.astype(bf16), widen)
        same = iota((rows_f, DH * heads), 0) % heads == iota((rows_f, DH * heads), 1) % heads
        repeated = jnp.concatenate(
            [jnp.where(same, wide[b * rows_f : (b + 1) * rows_f], 0.0) for b in range(blocks)], axis=1
        )
    w_rows = w_qkv.reshape(3, width * heads, DH)
    half = width * heads // 2

    def padded(part):
        return jnp.concatenate([part, jnp.zeros((rows - rows_f, DH), f32)], axis=0).astype(bf16)

    halved = jnp.concatenate([repeated[:, :half], repeated[:, half:]], axis=0).astype(bf16)
    w_qkv_copy(0).wait()
    w_halves = jnp.concatenate([w_rows[0, :half], w_rows[0, half:]], axis=1)
    cut = half // 2
    crossed = dot(halved[:, :cut], w_halves[:cut]) + dot(halved[:, cut:], w_halves[cut:])
    query = padded((crossed[:rows_f, :DH] + crossed[rows_f:, DH:]) * DH ** (-0.5))
    all_query[me] = query
    pl.semaphore_wait(barrier, n - 1 + nh - 1)

    def all_others(buffer, send_sem, recv_sem):
        return pltpu.make_async_remote_copy(
            src_ref=buffer.at[pl.ds(0, n - 1)], dst_ref=buffer.at[pl.ds(0, n - 1)],
            send_sem=send_sem, recv_sem=recv_sem,
            device_id={"req": lax.rem(me + 1, n)}, device_id_type=MESH,
        )

    def query_copy(slot, other):
        return pltpu.make_async_remote_copy(
            src_ref=all_query.at[slot], dst_ref=all_query.at[slot],
            send_sem=q_send, recv_sem=q_recv,
            device_id={"req": other}, device_id_type=MESH,
        )

    @functools.partial(each, n)
    def _(k):
        query_copy(me, lax.rem(me + k, n)).start()

    query_f = query[:rows_f]
    row = iota((rows_f, 1), 0)
    row_head, row_token = row % heads, row // heads
    memory_copy.wait()
    recalled = jnp.zeros((rows_f, DH), f32)
    for h in range(heads):
        recalled = jnp.where(row_head == h, dot(query_f, memory[h]), recalled)
    persist_copy.wait()
    col = iota((1, heads * NP), 1)
    score_persist = jnp.where(row_head == col // NP, dot_t(query_f, persist[:, :DH]), masked_score)

    for s in range(pieces):
        for copy in cache_copies(s):
            copy.wait()

    all_queries = all_others(all_query, q_send, q_recv)
    all_queries.wait_recv()

    col = iota((1, slots * heads), 1)
    same_head = row_head == col % heads
    col_slot = col // heads
    key_rows = keys.reshape(pieces, slots * heads, DH)
    value_rows = values.reshape(pieces, slots * heads, DH)
    owner_copy.wait()
    len_copy.wait()
    owners = [owner_ref[s] for s in range(pieces)]
    peaks, totals, sums = [], [], []
    gap = jnp.zeros((rows_f, DH), f32)
    for s in range(0, pieces, 2):
        pair = (s, s + 1)
        first, second = [all_query[owners[k]].astype(f32)[:rows_f] for k in pair]
        left = jnp.concatenate([first, gap], axis=0)
        right = jnp.concatenate([gap, second], axis=0)
        both = jnp.concatenate([left, right], axis=1).astype(bf16)
        scores = dot_t(both, jnp.concatenate([key_rows[k] for k in pair], axis=1))
        weights = []
        for k in pair:
            valid = same_head & (col_slot < len_ref[k])
            own_scores = jnp.where(valid, scores[(k - s) * rows_f : (k - s + 1) * rows_f], masked_score)
            peak = jnp.max(own_scores, axis=-1, keepdims=True)
            weight = jnp.where(valid, jnp.exp(own_scores - peak), 0.0)
            peaks.append(peak)
            totals.append(jnp.sum(weight, axis=-1, keepdims=True))
            weights.append(weight)
        weights = jnp.concatenate(weights, axis=0).astype(bf16)
        summed = dot(weights, jnp.concatenate([value_rows[k] for k in pair], axis=1))
        sums += [summed[:rows_f, :DH], summed[rows_f:, DH:]]

    eye = iota((rows_f, DH), 0) == iota((rows_f, DH), 1)
    zeros_tail = jnp.zeros((2, DH), f32)

    def as_row(column):
        return jnp.sum(jnp.where(eye, column, 0.0), axis=0, keepdims=True)

    def send_form(m, l, o):
        return jnp.concatenate([o] + three_terms(m) + three_terms(l) + [zeros_tail], axis=0).astype(bf16)

    same_owner = [[owners[s] == owners[k] for k in range(pieces)] for s in range(pieces)]
    shared = []
    for s in range(pieces):
        peak = peaks[s]
        for k in range(pieces):
            if k != s:
                peak = jnp.maximum(peak, jnp.where(same_owner[s][k], peaks[k], masked_score))
        shared.append(peak)
    peak_rows = [as_row(peak) for peak in shared]
    total_rows = []
    for s in range(pieces):
        factor = jnp.exp(peaks[s] - shared[s])
        total_rows.append(as_row(totals[s] * factor))
        sums[s] = sums[s] * factor
    for s in range(pieces):
        total, summed = total_rows[s], sums[s]
        for k in range(pieces):
            if k != s:
                total = total + jnp.where(same_owner[s][k], total_rows[k], 0.0)
                summed = summed + jnp.where(same_owner[s][k], sums[k], 0.0)
        made[s] = send_form(peak_rows[s], total, summed)
    nothing = jnp.zeros((1, DH), f32)
    made[pieces] = send_form(nothing + masked_score, nothing, jnp.zeros((rows_f, DH), f32))

    def message(r):
        which = jnp.int32(pieces)
        for s in range(pieces):
            which = jnp.where(owners[s] == r, s, which)
        return made[which]

    def partial_copy(mine, other):
        return pltpu.make_async_remote_copy(
            src_ref=outbox.at[other], dst_ref=inbox.at[mine],
            send_sem=p_send, recv_sem=p_recv,
            device_id={"req": other}, device_id_type=MESH,
        )

    @functools.partial(each, n)
    def _(k):
        other = lax.rem(me + k, n)
        outbox[other] = message(other)
        partial_copy(me, other).start()

    inbox[me] = message(me)

    w_qkv_copy(1).wait()
    w_qkv_copy(2).wait()
    whole = repeated.astype(bf16)
    w_new = jnp.concatenate([w_rows[1], w_rows[2]], axis=1)
    new = dot(whole[:, :half], w_new[:half]) + dot(whole[:, half:], w_new[half:])
    new_key, new_value = padded(new[:, :DH]), padded(new[:, DH:])
    col = iota((1, rows), 1)
    seen = (row_head == col % heads) & (col // heads <= row_token) & (col < Q * heads)
    score_new = jnp.where(seen, dot_t(query_f, new_key), masked_score)
    m_own = jnp.maximum(
        jnp.max(score_persist, axis=-1, keepdims=True), jnp.max(score_new, axis=-1, keepdims=True)
    )
    w_persist = jnp.exp(score_persist - m_own)
    w_new = jnp.exp(score_new - m_own)
    l_own = jnp.sum(w_persist, axis=-1, keepdims=True) + jnp.sum(w_new, axis=-1, keepdims=True)
    o_own = dot(w_persist.astype(bf16), persist[:, DH:]) + dot(w_new.astype(bf16), new_value)

    all_partials = all_others(inbox, p_send, p_recv)
    all_partials.wait_recv()

    got = inbox[...].astype(f32)
    tail = got[:, rows_f:]
    m_all = tail[:, 0:1] + (tail[:, 1:2] + tail[:, 2:3])
    l_all = tail[:, 3:4] + (tail[:, 4:5] + tail[:, 5:6])
    m_cache = jnp.max(m_all, axis=0)
    factor = jnp.exp(m_all - m_cache[None])
    l_cache = jnp.sum(l_all * factor, axis=0)

    def as_column(rows_):
        return jnp.sum(jnp.where(eye, rows_, 0.0), axis=-1, keepdims=True)

    o_cache = jnp.zeros((rows_f, DH), f32)
    for k in range(n):
        o_cache = o_cache + got[k, :rows_f] * as_column(factor[k])
    m_cache, l_cache = as_column(m_cache), as_column(l_cache)
    m = jnp.maximum(m_cache, m_own)
    scale_cache, scale_own = jnp.exp(m_cache - m), jnp.exp(m_own - m)
    total = l_cache * scale_cache + l_own * scale_own
    attended = (o_cache * scale_cache + o_own * scale_own) / total
    head_out = (attended + recalled).astype(bf16)

    target, source = iota((8 * heads, rows_f), 0), iota((8 * heads, rows_f), 1)
    pick = (target % 8 < Q) & (source == (target % 8) * heads + target // 8)
    by_head = dot(pick.astype(f32).astype(bf16), head_out)
    lanes = jnp.concatenate([by_head[8 * h : 8 * h + 8] for h in range(heads)], axis=1).astype(bf16)
    w_out_copy.wait()
    def half_copy(mine, other):
        return pltpu.make_async_remote_copy(
            src_ref=partial.at[other], dst_ref=halves.at[mine],
            send_sem=h_send.at[other], recv_sem=h_recv.at[mine],
            device_id={"head": other}, device_id_type=MESH,
        )

    def layer_part(k):
        start = pl.multiple_of(k * columns, columns)
        return dot(lanes, w_out[:, :, pl.ds(start, columns)].reshape(heads * DH, columns))

    @functools.partial(each, nh)
    def _(k):
        other = lax.rem(my_head + k, nh)
        partial[other] = layer_part(other)
        half_copy(my_head, other).start()

    halves[my_head] = layer_part(my_head)

    @functools.partial(each, nh)
    def _(k):
        other = lax.rem(my_head + k, nh)
        half_copy(other, other).wait_recv()

    out_ref[...] = jnp.sum(halves[...], axis=0)[:Q].astype(bf16)

    all_queries.wait_send()
    all_partials.wait_send()

    @functools.partial(each, nh)
    def _(k):
        half_copy(my_head, lax.rem(my_head + k, nh)).wait_send()


def shards(n, nh, tokens, norm_gain, w_qkv, persist_kv, memory, cache_kv, piece_owner, piece_len, w_out):
    heads = w_qkv.shape[1]
    pieces, slots = cache_kv.shape[:2]
    columns = w_out.shape[2] // nh
    rows_f = -(-(Q * heads - 8) // 16) * 16 + 8
    rows = rows_f + 8
    width = tokens.shape[1]
    if heads > 1:
        cache = cache_kv.reshape(pieces, slots, heads, 2, DH).transpose(0, 1, 3, 2, 4)
        cache_shape = (pieces, slots, heads, DH)
        w_qkv = w_qkv.reshape(width, heads, 3, DH).transpose(0, 2, 1, 3)
        w_shape = (3, width, heads, DH)
    else:
        cache = cache_kv.reshape(pieces, slots, 2 * DH)
        cache_shape = (pieces, slots, DH)
        w_qkv = w_qkv.reshape(width, 3 * DH)
        w_shape = (3, width, DH)
    vmem = pl.BlockSpec(memory_space=pltpu.VMEM)
    hbm = pl.BlockSpec(memory_space=pltpu.HBM)
    dma = pltpu.SemaphoreType.DMA
    return pl.pallas_call(
        functools.partial(kernel, n, nh, heads, pieces, rows_f, rows),
        out_shape=pltpu.VMEM((Q, columns), bf16),
        in_specs=[hbm] * 9,
        out_specs=vmem,
        scratch_shapes=[
            pltpu.SMEM((pieces,), jnp.int32),
            pltpu.SMEM((pieces,), jnp.int32),
            pltpu.VMEM((Q, width), bf16),
            pltpu.VMEM((1, width), f32),
            pltpu.VMEM(w_shape, bf16),
            pltpu.VMEM((heads * NP, 2 * DH), bf16),
            pltpu.VMEM(cache_shape, bf16),
            pltpu.VMEM(cache_shape, bf16),
            pltpu.VMEM((heads, DH, DH), bf16),
            pltpu.VMEM((heads, DH, nh * columns), bf16),
            pltpu.VMEM((n, rows, DH), bf16),
            pltpu.VMEM((pieces + 1, rows, DH), bf16),
            pltpu.VMEM((n, rows, DH), bf16),
            pltpu.VMEM((n, rows, DH), bf16),
            pltpu.VMEM((nh, 8, columns), f32),
            pltpu.VMEM((nh, 8, columns), f32),
            dma((pieces,)), dma((pieces,)), dma((7,)), dma((3,)),
            dma, dma, dma, dma, dma((nh,)), dma((nh,)),
        ],
        compiler_params=pltpu.CompilerParams(
            collective_id=0, has_side_effects=True, vmem_limit_bytes=62 * 2**20
        ),
        cost_estimate=pl.CostEstimate(flops=100_000_000, bytes_accessed=10_000_000, transcendentals=500_000),
    )(
        piece_owner, piece_len, tokens, norm_gain.reshape(1, width), w_qkv,
        persist_kv.reshape(heads * NP, 2 * DH), cache, memory.reshape(heads, DH, DH), w_out,
    )


def solution(mesh):
    in_specs = (
        P("req", None),
        P(),
        P(None, "head", None),
        P("head", None, None),
        P("req", "head", None, None),
        P("req", None, "head", None),
        P("req"),
        P("req"),
        P("head", None, None),
    )
    n, nh = mesh.shape["req"], mesh.shape["head"]
    return jax.shard_map(
        functools.partial(shards, n, nh), mesh=mesh, in_specs=in_specs, out_specs=P("req", "head"), check_vma=False
    )
```

```python
import functools

import jax
import jax.numpy as jnp
from jax import lax
from jax.experimental import pallas as pl
from jax.experimental.pallas import tpu as pltpu
from jax.sharding import PartitionSpec as P

DH = 128
NP = 16
Q = 5
MESH = pl.DeviceIdType.MESH

masked_score = -1e30
norm_eps = 1e-06
f32 = jnp.float32
bf16 = jnp.bfloat16


def dot(a, b):
    return jnp.dot(a, b, preferred_element_type=f32)


def dot_t(a, b):
    return lax.dot_general(a, b, (((1,), (1,)), ((), ())), preferred_element_type=f32)


def iota(shape, dim):
    return lax.broadcasted_iota(jnp.int32, shape, dim)


def each(count, body):
    if count <= 16:
        for k in range(1, count):
            body(k)
    else:
        pl.loop(1, count)(body)


def three_terms(x):
    high = x.astype(bf16).astype(f32)
    middle = (x - high).astype(bf16).astype(f32)
    return [high, middle, x - high - middle]


def kernel(
    n, nh, heads, pieces, rows_f, rows,
    owner_hbm, len_hbm, tokens_ref, gain_ref, w_qkv_ref, persist_ref, cache_ref, memory_ref, w_out_ref,
    out_ref,
    owner_ref, len_ref, tokens, gain, w_qkv, persist, keys, values, memory, w_out,
    all_query, made, outbox, inbox, partial, halves,
    key_sem, value_sem, weight_sem, w_qkv_sem, q_send, q_recv, p_send, p_recv, h_send, h_recv,
):
    me = lax.axis_index("req")
    my_head = lax.axis_index("head")
    columns = partial.shape[-1]
    slots = cache_ref.shape[1]

    barrier = pltpu.get_barrier_semaphore()

    @functools.partial(each, n)
    def _(k):
        pl.semaphore_signal(barrier, inc=1, device_id={"req": lax.rem(me + k, n)}, device_id_type=MESH)

    @functools.partial(each, nh)
    def _(k):
        pl.semaphore_signal(barrier, inc=1, device_id={"head": lax.rem(my_head + k, nh)}, device_id_type=MESH)

    def cache_copies(s):
        if heads > 1:
            key_view, value_view = cache_ref.at[s, :, 0], cache_ref.at[s, :, 1]
        else:
            key_view, value_view = cache_ref.at[s, :, pl.ds(0, DH)], cache_ref.at[s, :, pl.ds(DH, DH)]
        return (
            pltpu.make_async_copy(key_view, keys.at[s], key_sem.at[s]),
            pltpu.make_async_copy(value_view, values.at[s], value_sem.at[s]),
        )

    def w_qkv_copy(c):
        view = w_qkv_ref.at[:, c] if heads > 1 else w_qkv_ref.at[:, pl.ds(c * DH, DH)]
        return pltpu.make_async_copy(view, w_qkv.at[c], w_qkv_sem.at[c])

    tokens_copy = pltpu.make_async_copy(tokens_ref, tokens, weight_sem.at[0])
    gain_copy = pltpu.make_async_copy(gain_ref, gain, weight_sem.at[1])
    persist_copy = pltpu.make_async_copy(persist_ref, persist, weight_sem.at[2])
    memory_copy = pltpu.make_async_copy(memory_ref, memory, weight_sem.at[3])
    w_out_copy = pltpu.make_async_copy(w_out_ref, w_out, weight_sem.at[4])
    tokens_copy.start()
    gain_copy.start()
    for c in range(3):
        w_qkv_copy(c).start()

    owner_copy = pltpu.make_async_copy(owner_hbm, owner_ref, weight_sem.at[5])
    len_copy = pltpu.make_async_copy(len_hbm, len_ref, weight_sem.at[6])
    owner_copy.start()
    len_copy.start()
    persist_copy.start()
    memory_copy.start()
    for s in range(pieces):
        for copy in cache_copies(s):
            copy.start()
    w_out_copy.start()

    tokens_copy.wait()
    gain_copy.wait()
    x = tokens[...].astype(f32)
    width = x.shape[1]
    normed = (x * lax.rsqrt(jnp.mean(x * x, axis=-1, keepdims=True) + norm_eps) * gain[...]).astype(bf16)
    spread = (iota((rows_f, Q), 0) // heads == iota((rows_f, Q), 1)).astype(f32).astype(bf16)
    repeated = dot(spread, normed)
    if heads > 1:
        blocks = width // DH
        stacked = jnp.concatenate([repeated[:, b * DH : (b + 1) * DH] for b in range(blocks)], axis=0)
        widen = (iota((DH, DH * heads), 0) == iota((DH, DH * heads), 1) // heads).astype(f32).astype(bf16)
        wide = dot(stacked.astype(bf16), widen)
        same = iota((rows_f, DH * heads), 0) % heads == iota((rows_f, DH * heads), 1) % heads
        repeated = jnp.concatenate(
            [jnp.where(same, wide[b * rows_f : (b + 1) * rows_f], 0.0) for b in range(blocks)], axis=1
        )
    w_rows = w_qkv.reshape(3, width * heads, DH)
    half = width * heads // 2

    def padded(part):
        return jnp.concatenate([part, jnp.zeros((rows - rows_f, DH), f32)], axis=0).astype(bf16)

    halved = jnp.concatenate([repeated[:, :half], repeated[:, half:]], axis=0).astype(bf16)
    w_qkv_copy(0).wait()
    w_halves = jnp.concatenate([w_rows[0, :half], w_rows[0, half:]], axis=1)
    cut = half // 2
    crossed = dot(halved[:, :cut], w_halves[:cut]) + dot(halved[:, cut:], w_halves[cut:])
    query = padded((crossed[:rows_f, :DH] + crossed[rows_f:, DH:]) * DH ** (-0.5))
    all_query[me] = query
    pl.semaphore_wait(barrier, n - 1 + nh - 1)

    def all_others(buffer, send_sem, recv_sem):
        return pltpu.make_async_remote_copy(
            src_ref=buffer.at[pl.ds(0, n - 1)], dst_ref=buffer.at[pl.ds(0, n - 1)],
            send_sem=send_sem, recv_sem=recv_sem,
            device_id={"req": lax.rem(me + 1, n)}, device_id_type=MESH,
        )

    def query_copy(slot, other):
        return pltpu.make_async_remote_copy(
            src_ref=all_query.at[slot], dst_ref=all_query.at[slot],
            send_sem=q_send, recv_sem=q_recv,
            device_id={"req": other}, device_id_type=MESH,
        )

    @functools.partial(each, n)
    def _(k):
        query_copy(me, lax.rem(me + k, n)).start()

    query_f = query[:rows_f]
    row = iota((rows_f, 1), 0)
    row_head, row_token = row % heads, row // heads
    memory_copy.wait()
    recalled = jnp.zeros((rows_f, DH), f32)
    for h in range(heads):
        recalled = jnp.where(row_head == h, dot(query_f, memory[h]), recalled)
    persist_copy.wait()
    col = iota((1, heads * NP), 1)
    score_persist = jnp.where(row_head == col // NP, dot_t(query_f, persist[:, :DH]), masked_score)

    for s in range(pieces):
        for copy in cache_copies(s):
            copy.wait()

    all_queries = all_others(all_query, q_send, q_recv)
    all_queries.wait_recv()

    col = iota((1, slots * heads), 1)
    same_head = row_head == col % heads
    col_slot = col // heads
    key_rows = keys.reshape(pieces, slots * heads, DH)
    value_rows = values.reshape(pieces, slots * heads, DH)
    owner_copy.wait()
    len_copy.wait()
    owners = [owner_ref[s] for s in range(pieces)]
    peaks, totals, sums = [], [], []
    gap = jnp.zeros((rows_f, DH), f32)
    for s in range(0, pieces, 2):
        pair = (s, s + 1)
        first, second = [all_query[owners[k]].astype(f32)[:rows_f] for k in pair]
        left = jnp.concatenate([first, gap], axis=0)
        right = jnp.concatenate([gap, second], axis=0)
        both = jnp.concatenate([left, right], axis=1).astype(bf16)
        scores = dot_t(both, jnp.concatenate([key_rows[k] for k in pair], axis=1))
        weights = []
        for k in pair:
            valid = same_head & (col_slot < len_ref[k])
            own_scores = jnp.where(valid, scores[(k - s) * rows_f : (k - s + 1) * rows_f], masked_score)
            peak = jnp.max(own_scores, axis=-1, keepdims=True)
            weight = jnp.where(valid, jnp.exp(own_scores - peak), 0.0)
            peaks.append(peak)
            totals.append(jnp.sum(weight, axis=-1, keepdims=True))
            weights.append(weight)
        weights = jnp.concatenate(weights, axis=0).astype(bf16)
        summed = dot(weights, jnp.concatenate([value_rows[k] for k in pair], axis=1))
        sums += [summed[:rows_f, :DH], summed[rows_f:, DH:]]

    eye = iota((rows_f, DH), 0) == iota((rows_f, DH), 1)
    zeros_tail = jnp.zeros((2, DH), f32)

    def as_row(column):
        return jnp.sum(jnp.where(eye, column, 0.0), axis=0, keepdims=True)

    def send_form(m, l, o):
        return jnp.concatenate([o] + three_terms(m) + three_terms(l) + [zeros_tail], axis=0).astype(bf16)

    same_owner = [[owners[s] == owners[k] for k in range(pieces)] for s in range(pieces)]
    shared = []
    for s in range(pieces):
        peak = peaks[s]
        for k in range(pieces):
            if k != s:
                peak = jnp.maximum(peak, jnp.where(same_owner[s][k], peaks[k], masked_score))
        shared.append(peak)
    peak_rows = [as_row(peak) for peak in shared]
    total_rows = []
    for s in range(pieces):
        factor = jnp.exp(peaks[s] - shared[s])
        total_rows.append(as_row(totals[s] * factor))
        sums[s] = sums[s] * factor
    for s in range(pieces):
        total, summed = total_rows[s], sums[s]
        for k in range(pieces):
            if k != s:
                total = total + jnp.where(same_owner[s][k], total_rows[k], 0.0)
                summed = summed + jnp.where(same_owner[s][k], sums[k], 0.0)
        made[s] = send_form(peak_rows[s], total, summed)
    nothing = jnp.zeros((1, DH), f32)
    made[pieces] = send_form(nothing + masked_score, nothing, jnp.zeros((rows_f, DH), f32))

    def message(r):
        which = jnp.int32(pieces)
        for s in range(pieces):
            which = jnp.where(owners[s] == r, s, which)
        return made[which]

    def partial_copy(mine, other):
        return pltpu.make_async_remote_copy(
            src_ref=outbox.at[other], dst_ref=inbox.at[mine],
            send_sem=p_send, recv_sem=p_recv,
            device_id={"req": other}, device_id_type=MESH,
        )

    @functools.partial(each, n)
    def _(k):
        other = lax.rem(me + k, n)
        outbox[other] = message(other)
        partial_copy(me, other).start()

    inbox[me] = message(me)

    w_qkv_copy(1).wait()
    w_qkv_copy(2).wait()
    whole = repeated.astype(bf16)
    w_new = jnp.concatenate([w_rows[1], w_rows[2]], axis=1)
    new = dot(whole[:, :half], w_new[:half]) + dot(whole[:, half:], w_new[half:])
    new_key, new_value = padded(new[:, :DH]), padded(new[:, DH:])
    col = iota((1, rows), 1)
    seen = (row_head == col % heads) & (col // heads <= row_token) & (col < Q * heads)
    score_new = jnp.where(seen, dot_t(query_f, new_key), masked_score)
    m_own = jnp.maximum(
        jnp.max(score_persist, axis=-1, keepdims=True), jnp.max(score_new, axis=-1, keepdims=True)
    )
    w_persist = jnp.exp(score_persist - m_own)
    w_new = jnp.exp(score_new - m_own)
    l_own = jnp.sum(w_persist, axis=-1, keepdims=True) + jnp.sum(w_new, axis=-1, keepdims=True)
    o_own = dot(w_persist.astype(bf16), persist[:, DH:]) + dot(w_new.astype(bf16), new_value)

    all_partials = all_others(inbox, p_send, p_recv)
    all_partials.wait_recv()

    got = inbox[...].astype(f32)
    tail = got[:, rows_f:]
    m_all = tail[:, 0:1] + (tail[:, 1:2] + tail[:, 2:3])
    l_all = tail[:, 3:4] + (tail[:, 4:5] + tail[:, 5:6])
    m_cache = jnp.max(m_all, axis=0)
    factor = jnp.exp(m_all - m_cache[None])
    l_cache = jnp.sum(l_all * factor, axis=0)

    def as_column(rows_):
        return jnp.sum(jnp.where(eye, rows_, 0.0), axis=-1, keepdims=True)

    o_cache = jnp.zeros((rows_f, DH), f32)
    for k in range(n):
        o_cache = o_cache + got[k, :rows_f] * as_column(factor[k])
    m_cache, l_cache = as_column(m_cache), as_column(l_cache)
    m = jnp.maximum(m_cache, m_own)
    scale_cache, scale_own = jnp.exp(m_cache - m), jnp.exp(m_own - m)
    total = l_cache * scale_cache + l_own * scale_own
    attended = (o_cache * scale_cache + o_own * scale_own) / total
    head_out = (attended + recalled).astype(bf16)

    target, source = iota((8 * heads, rows_f), 0), iota((8 * heads, rows_f), 1)
    pick = (target % 8 < Q) & (source == (target % 8) * heads + target // 8)
    by_head = dot(pick.astype(f32).astype(bf16), head_out)
    lanes = jnp.concatenate([by_head[8 * h : 8 * h + 8] for h in range(heads)], axis=1).astype(bf16)
    w_out_copy.wait()
    def half_copy(mine, other):
        return pltpu.make_async_remote_copy(
            src_ref=partial.at[other], dst_ref=halves.at[mine],
            send_sem=h_send.at[other], recv_sem=h_recv.at[mine],
            device_id={"head": other}, device_id_type=MESH,
        )

    def layer_part(k):
        start = pl.multiple_of(k * columns, columns)
        return dot(lanes, w_out[:, :, pl.ds(start, columns)].reshape(heads * DH, columns))

    @functools.partial(each, nh)
    def _(k):
        other = lax.rem(my_head + k, nh)
        partial[other] = layer_part(other)
        half_copy(my_head, other).start()

    halves[my_head] = layer_part(my_head)

    @functools.partial(each, nh)
    def _(k):
        other = lax.rem(my_head + k, nh)
        half_copy(other, other).wait_recv()

    out_ref[...] = jnp.sum(halves[...], axis=0)[:Q].astype(bf16)

    all_queries.wait_send()
    all_partials.wait_send()

    @functools.partial(each, nh)
    def _(k):
        half_copy(my_head, lax.rem(my_head + k, nh)).wait_send()


def shards(n, nh, tokens, norm_gain, w_qkv, persist_kv, memory, cache_kv, piece_owner, piece_len, w_out):
    heads = w_qkv.shape[1]
    pieces, slots = cache_kv.shape[:2]
    columns = w_out.shape[2] // nh
    rows_f = -(-(Q * heads - 8) // 16) * 16 + 8
    rows = rows_f + 8
    width = tokens.shape[1]
    if heads > 1:
        cache = cache_kv.reshape(pieces, slots, heads, 2, DH).transpose(0, 1, 3, 2, 4)
        cache_shape = (pieces, slots, heads, DH)
        w_qkv = w_qkv.reshape(width, heads, 3, DH).transpose(0, 2, 1, 3)
        w_shape = (3, width, heads, DH)
    else:
        cache = cache_kv.reshape(pieces, slots, 2 * DH)
        cache_shape = (pieces, slots, DH)
        w_qkv = w_qkv.reshape(width, 3 * DH)
        w_shape = (3, width, DH)
    vmem = pl.BlockSpec(memory_space=pltpu.VMEM)
    hbm = pl.BlockSpec(memory_space=pltpu.HBM)
    dma = pltpu.SemaphoreType.DMA
    return pl.pallas_call(
        functools.partial(kernel, n, nh, heads, pieces, rows_f, rows),
        out_shape=pltpu.VMEM((Q, columns), bf16),
        in_specs=[hbm] * 9,
        out_specs=vmem,
        scratch_shapes=[
            pltpu.SMEM((pieces,), jnp.int32),
            pltpu.SMEM((pieces,), jnp.int32),
            pltpu.VMEM((Q, width), bf16),
            pltpu.VMEM((1, width), f32),
            pltpu.VMEM(w_shape, bf16),
            pltpu.VMEM((heads * NP, 2 * DH), bf16),
            pltpu.VMEM(cache_shape, bf16),
            pltpu.VMEM(cache_shape, bf16),
            pltpu.VMEM((heads, DH, DH), bf16),
            pltpu.VMEM((heads, DH, nh * columns), bf16),
            pltpu.VMEM((n, rows, DH), bf16),
            pltpu.VMEM((pieces + 1, rows, DH), bf16),
            pltpu.VMEM((n, rows, DH), bf16),
            pltpu.VMEM((n, rows, DH), bf16),
            pltpu.VMEM((nh, 8, columns), f32),
            pltpu.VMEM((nh, 8, columns), f32),
            dma((pieces,)), dma((pieces,)), dma((7,)), dma((3,)),
            dma, dma, dma, dma, dma((nh,)), dma((nh,)),
        ],
        compiler_params=pltpu.CompilerParams(
            collective_id=0, has_side_effects=True, vmem_limit_bytes=62 * 2**20
        ),
        cost_estimate=pl.CostEstimate(flops=100_000_000, bytes_accessed=10_000_000, transcendentals=500_000),
    )(
        piece_owner, piece_len, tokens, norm_gain.reshape(1, width), w_qkv,
        persist_kv.reshape(heads * NP, 2 * DH), cache, memory.reshape(heads, DH, DH), w_out,
    )


def solution(mesh):
    in_specs = (
        P("req", None),
        P(),
        P(None, "head", None),
        P("head", None, None),
        P("req", "head", None, None),
        P("req", None, "head", None),
        P("req"),
        P("req"),
        P("head", None, None),
    )
    n, nh = mesh.shape["req"], mesh.shape["head"]
    return jax.shard_map(
        functools.partial(shards, n, nh), mesh=mesh, in_specs=in_specs, out_specs=P("req", "head"), check_vma=False
    )
```
